32 devices in a mesh: batch: 8 (over y, x, core), mp: 4 (over z).
Axes of the slice: x: 2, y: 2, z: 4, core: 2. Of those that a mesh axis runs over, the one named last changes fastest.
Arguments:
- residual: bfloat16 [8, 64, 8192], P('batch', None, 'mp'), may hold values from -6 to 6
- query_states: bfloat16 [8, 64, 4096], P('batch', None, 'mp')
- key_states: bfloat16 [8, 64, 512], P('batch')
- value_states: bfloat16 [8, 64, 512], P('batch'), may hold values from -6 to 6
- prompt_perm: int32 [8], replicated, may hold values from 0 to 7, each once
- ablated_heads: int32 [8], replicated, may hold values from 0 to 31, as said below
- out_weight: bfloat16 [4096, 8192], P('batch', 'mp'), may hold values from -0.09375 to 0.09375
- rms_gain: float32 [8192], P('mp'), may hold values from 0.1 to 1.9
- gate_weight: bfloat16 [8192, 14336], P('mp', 'batch'), may hold values from -0.0625 to 0.0625
- up_weight: bfloat16 [8192, 14336], P('mp', 'batch'), may hold values from -0.0625 to 0.0625
- down_weight: bfloat16 [14336, 8192], P('batch', 'mp'), may hold values from -0.046875 to 0.046875
Outputs:
- attn_out: bfloat16 [8, 64, 8192], P('batch', None, 'mp')
- mlp_out: bfloat16 [8, 64, 8192], P('batch', None, 'mp')
The draws below stay inside these ranges and needn't reach their ends.
Inputs may be any that keep to these rules, and one draw needn't show every extreme that they name: `prompt_perm`: each prompt index appears exactly once. `ablated_heads`: 8 different head indices in any order, one of them 32 - 1.
All inputs are finite; a program needn't handle non-finite values.
Results may differ from the reference program's by a relative error of at most 0.035.
Values may be sent and summed in bfloat16 or wider, within the bound.
A program may use at most 128 MiB of HBM per device.

```python
import math
import jax
import jax.numpy as jnp
from jax import lax

D = 8192
HEADS = 32
KV = 4
HD = 128
FF = 14336
ABLATED = 8
SEQ = 64
PROMPTS = 8
N_BATCH = 8


def key_table(key):
    return jax.random.normal(jax.random.fold_in(key, 11), (PROMPTS, SEQ, KV * HD), jnp.float32)


def draw_key_states(key, part):
    return key_table(key).astype(jnp.bfloat16)


def draw_query_states(key, part):
    base = jax.random.normal(jax.random.fold_in(key, 23), (PROMPTS, SEQ, HEADS * HD), jnp.float32)
    return base.astype(jnp.bfloat16)


def draw_ablated_heads(key, part):
    others = jax.random.permutation(jax.random.fold_in(key, 37), HEADS - 1)[:ABLATED - 1].astype(jnp.int32)
    listed = jnp.concatenate([others, jnp.full((1,), HEADS - 1, jnp.int32)])
    order = jax.random.permutation(jax.random.fold_in(key, 41), ABLATED)
    return jnp.take(listed, order).astype(jnp.int32)


def block_levels(stream_key, extent, cuts, low, high):
    level, own = 1.0, jax.random.fold_in(stream_key, 6)
    for axis_at, shards_of in cuts:
        heights = jnp.exp(jax.random.uniform(jax.random.fold_in(own, axis_at), (shards_of,), jnp.float32, low / len(cuts), high / len(cuts)))
        level = level * jnp.repeat(heights, extent[axis_at] // shards_of).reshape([-1 if axis == axis_at else 1 for axis in range(len(extent))])
    return level


def normal_values(rng, shape, scale, most, shards=(), held_as=jnp.bfloat16):
    factor_of = block_levels(rng, shape, shards, -0.22, 0.18) if shards else 1.0
    result = jax.random.normal(rng, shape, jnp.float32) * scale * factor_of
    return jnp.minimum(jnp.maximum(result, -most), most).astype(held_as)


def setup_inputs(seed: int = 0) -> dict:
    seeds = jax.random.split(jax.random.key(seed), 12)
    residual = normal_values(seeds[0], (PROMPTS, SEQ, D), 1.0, 6.0, ((0, 8), (2, 4)))
    query_states = draw_query_states(jax.random.fold_in(seeds[11], 71), 0)
    key_states = draw_key_states(jax.random.fold_in(seeds[11], 71), 0)
    value_states = normal_values(seeds[3], (PROMPTS, SEQ, KV * HD), 1.0, 6.0, ((0, 8),))
    prompt_perm = jax.random.permutation(seeds[4], PROMPTS).astype(jnp.int32)
    ablated_heads = draw_ablated_heads(jax.random.fold_in(seeds[11], 71), 0)
    out_weight = normal_values(seeds[6], (HEADS * HD, D), (HEADS * HD) ** -0.5, 0.09375, ((0, 8), (1, 4)))
    rms_gain = jnp.clip(1.0 + 0.18 * jax.random.normal(seeds[7], (D,), jnp.float32), 0.1, 1.9)
    gate_weight = normal_values(seeds[8], (D, FF), D ** -0.5, 0.0625, ((0, 4), (1, 8)))
    up_weight = normal_values(seeds[9], (D, FF), D ** -0.5, 0.0625, ((0, 4), (1, 8)))
    down_weight = normal_values(seeds[10], (FF, D), FF ** -0.5, 0.046875, ((0, 8), (1, 4)))
    return dict(residual=residual, query_states=query_states, key_states=key_states, value_states=value_states, prompt_perm=prompt_perm, ablated_heads=ablated_heads, out_weight=out_weight, rms_gain=rms_gain, gate_weight=gate_weight, up_weight=up_weight, down_weight=down_weight)


def attend_prompt(triple):
    query_rows, key_rows, value_rows = triple
    grouped = query_rows.astype(jnp.float32).reshape(SEQ, KV, HEADS // KV, HD)
    key_float = key_rows.astype(jnp.float32).reshape(SEQ, KV, HD)
    value_float = value_rows.astype(jnp.float32).reshape(SEQ, KV, HD)
    scores = jnp.einsum('skgd,tkd->kgst', grouped, key_float) / math.sqrt(HD)
    positions = jnp.arange(SEQ)
    causal = positions[:, None] >= positions[None, :]
    scores = jnp.where(causal, scores, -1e+30)
    highest = lax.optimization_barrier(jnp.max(scores, axis=-1, keepdims=True))
    weights = jnp.exp(scores - highest)
    probability = (weights / lax.optimization_barrier(jnp.sum(weights, axis=-1, keepdims=True))).astype(jnp.bfloat16)
    mixed_heads = jnp.einsum('kgst,tkd->skgd', probability.astype(jnp.float32), value_float)
    return mixed_heads.astype(jnp.bfloat16).reshape(SEQ, HEADS * HD)

def reference(residual, query_states, key_states, value_states, prompt_perm, ablated_heads, out_weight, rms_gain, gate_weight, up_weight, down_weight):
    head_rows = lax.map(attend_prompt, (query_states, key_states, value_states))
    stacked = head_rows.reshape(PROMPTS, SEQ, HEADS, HD)
    swapped = jnp.take(stacked, prompt_perm, axis=0)
    chosen = jnp.any(jnp.arange(HEADS)[:, None] == ablated_heads[None, :], axis=1)
    ablated = jnp.where(chosen[None, None, :, None], swapped, stacked).reshape(PROMPTS * SEQ, HEADS * HD)
    attn_float = jnp.dot(ablated, out_weight, preferred_element_type=jnp.float32)
    attn_out = attn_float.astype(jnp.bfloat16)
    hidden_state = residual.reshape(PROMPTS * SEQ, D).astype(jnp.float32) + attn_float
    inverse = lax.rsqrt(lax.optimization_barrier(jnp.mean(hidden_state * hidden_state, axis=1)) + 1e-05)
    normed = (hidden_state * inverse[:, None] * rms_gain.astype(jnp.float32)[None, :]).astype(jnp.bfloat16)
    gate_part = jnp.dot(normed, gate_weight, preferred_element_type=jnp.float32)
    up_part = jnp.dot(normed, up_weight, preferred_element_type=jnp.float32)
    hidden = (jax.nn.silu(gate_part) * up_part).astype(jnp.bfloat16)
    slice_width = FF // N_BATCH
    slices = hidden.reshape(PROMPTS * SEQ, N_BATCH, slice_width).transpose(1, 0, 2)
    blocks = down_weight.reshape(N_BATCH, slice_width, D)

    def add_part(running, operands):
        part_value = jnp.dot(operands[0], operands[1], preferred_element_type=jnp.float32).astype(jnp.bfloat16)
        return (running + part_value.astype(jnp.float32), None)
    running, unused = lax.scan(add_part, jnp.zeros((PROMPTS * SEQ, D), jnp.float32), (slices, blocks))
    return (attn_out.reshape(PROMPTS, SEQ, D), running.astype(jnp.bfloat16).reshape(PROMPTS, SEQ, D))
```

```python
import functools
import math

import jax
import jax.numpy as jnp
from jax import lax
from jax.experimental import pallas as pl
from jax.experimental.pallas import tpu as pltpu
from jax.sharding import PartitionSpec as P

D = 8192
HEADS = 32
KV = 4
HD = 128
ABLATED = 8


def heads_kernel(q_ref, k_ref, v_ref, o_ref):
    length = q_ref.shape[1]
    rows = lax.broadcasted_iota(jnp.int32, (length, length), 0)
    cols = lax.broadcasted_iota(jnp.int32, (length, length), 1)
    causal = rows >= cols
    for head in range(q_ref.shape[2] // HD):
        at = slice(head * HD, (head + 1) * HD)
        kv = slice(head * k_ref.shape[2] * HD // q_ref.shape[2] // HD * HD, None)
        kv = slice(kv.start, kv.start + HD)
        scores = lax.dot_general(
            q_ref[0, :, at],
            k_ref[0, :, kv],
            (((1,), (1,)), ((), ())),
            preferred_element_type=jnp.float32,
        ) / math.sqrt(HD)
        scores = jnp.where(causal, scores, -1e30)
        highest = jnp.max(scores, axis=-1, keepdims=True)
        weights = jnp.exp(scores - highest)
        probability = (weights / jnp.sum(weights, axis=-1, keepdims=True)).astype(jnp.bfloat16)
        o_ref[0, :, at] = jnp.dot(
            probability, v_ref[0, :, kv], preferred_element_type=jnp.float32
        ).astype(jnp.bfloat16)


def local_heads(query_states, key_states, value_states):
    prompts_here, length, columns = query_states.shape
    head_count = columns // HD
    group = HEADS // KV
    kv_count = max(1, head_count // group)
    first = lax.axis_index("mp") * head_count // group
    keys = lax.dynamic_slice_in_dim(key_states, first * HD, kv_count * HD, axis=2)
    values = lax.dynamic_slice_in_dim(value_states, first * HD, kv_count * HD, axis=2)
    spec = lambda width: pl.BlockSpec((1, length, width), lambda i: (i, 0, 0))
    return pl.pallas_call(
        heads_kernel,
        grid=(prompts_here,),
        in_specs=[spec(columns), spec(kv_count * HD), spec(kv_count * HD)],
        out_specs=spec(columns),
        out_shape=jax.ShapeDtypeStruct((prompts_here, length, columns), jnp.bfloat16),
    )(query_states, keys, values)


def body(
    residual,
    query_states,
    key_states,
    value_states,
    prompt_perm,
    ablated_heads,
    out_weight,
    rms_gain,
    gate_weight,
    up_weight,
    down_weight,
):
    prompts_here, length, model_cols = residual.shape
    local_rows = prompts_here * length
    batches = lax.axis_size("batch")
    head_block = local_heads(query_states, key_states, value_states)
    all_heads = lax.all_gather(head_block, "mp", axis=2, tiled=True)
    owned_cols = out_weight.shape[0]
    by_owner = all_heads.reshape(local_rows, batches, owned_cols).transpose(1, 0, 2)
    mine = lax.all_to_all(by_owner, "batch", 0, 0, tiled=True)
    prompts = batches * prompts_here
    mine = mine.reshape(prompts, length, owned_cols)
    swapped = jnp.concatenate(
        [lax.dynamic_slice_in_dim(mine, prompt_perm[p], 1, axis=0) for p in range(prompts)], axis=0
    )
    head_of_col = (lax.axis_index("batch") * owned_cols + jnp.arange(owned_cols)) // HD
    chosen = jnp.any(head_of_col[:, None] == ablated_heads[None, :], axis=1)
    ablated = jnp.where(chosen[None, None, :], swapped, mine).reshape(prompts * length, owned_cols)
    attn_part = jnp.dot(ablated, out_weight, preferred_element_type=jnp.float32)
    attn_sum = lax.psum_scatter(
        attn_part.astype(jnp.bfloat16), "batch", scatter_dimension=0, tiled=True
    )
    attn_float = attn_sum.astype(jnp.float32)
    attn_out = attn_sum
    hidden_state = residual.reshape(local_rows, model_cols).astype(jnp.float32) + attn_float
    squares = lax.psum(jnp.sum(hidden_state * hidden_state, axis=1), "mp")
    inverse = lax.rsqrt(squares / D + 1e-05)
    normed = (hidden_state * inverse[:, None] * rms_gain[None, :]).astype(jnp.bfloat16)
    block_rows = lax.all_gather(normed, "batch", axis=0, tiled=True)
    gate_part = jnp.dot(block_rows, gate_weight, preferred_element_type=jnp.float32)
    up_part = jnp.dot(block_rows, up_weight, preferred_element_type=jnp.float32)
    gate = lax.psum_scatter(
        gate_part.astype(jnp.bfloat16), "mp", scatter_dimension=0, tiled=True
    ).astype(jnp.float32)
    up = lax.psum_scatter(
        up_part.astype(jnp.bfloat16), "mp", scatter_dimension=0, tiled=True
    ).astype(jnp.float32)
    hidden = (jax.nn.silu(gate) * up).astype(jnp.bfloat16)
    hidden = lax.all_gather(hidden, "mp", axis=0, tiled=True)
    mlp_float = lax.psum_scatter(
        jnp.dot(hidden, down_weight, preferred_element_type=jnp.float32).astype(jnp.bfloat16),
        "batch",
        scatter_dimension=0,
        tiled=True,
    )
    return (
        attn_out.reshape(prompts_here, length, model_cols),
        mlp_float.reshape(prompts_here, length, model_cols),
    )


def solution(mesh):
    placed = (
        P("batch", None, "mp"),
        P("batch", None, "mp"),
        P("batch", None, None),
        P("batch", None, None),
        P(),
        P(),
        P("batch", "mp"),
        P("mp"),
        P("mp", "batch"),
        P("mp", "batch"),
        P("batch", "mp"),
    )
    return jax.shard_map(
        body,
        mesh=mesh,
        in_specs=placed,
        out_specs=(P("batch", None, "mp"), P("batch", None, "mp")),
        check_vma=False,
    )
```

```python
import functools
import functools
import math

import jax
import jax.numpy as jnp
from jax import lax
from jax.experimental import pallas as pl
from jax.experimental.pallas import tpu as pltpu
from jax.sharding import PartitionSpec as P

D = 8192
HEADS = 32
KV = 4
HD = 128
ABLATED = 8


def heads_kernel(q_ref, k_ref, v_ref, o_ref):
    length = q_ref.shape[1]
    rows = lax.broadcasted_iota(jnp.int32, (length, length), 0)
    cols = lax.broadcasted_iota(jnp.int32, (length, length), 1)
    causal = rows >= cols
    for head in range(q_ref.shape[2] // HD):
        at = slice(head * HD, (head + 1) * HD)
        kv = slice(head * k_ref.shape[2] * HD // q_ref.shape[2] // HD * HD, None)
        kv = slice(kv.start, kv.start + HD)
        scores = lax.dot_general(
            q_ref[0, :, at],
            k_ref[0, :, kv],
            (((1,), (1,)), ((), ())),
            preferred_element_type=jnp.float32,
        ) / math.sqrt(HD)
        scores = jnp.where(causal, scores, -1e30)
        highest = jnp.max(scores, axis=-1, keepdims=True)
        weights = jnp.exp(scores - highest)
        probability = (weights / jnp.sum(weights, axis=-1, keepdims=True)).astype(jnp.bfloat16)
        o_ref[0, :, at] = jnp.dot(
            probability, v_ref[0, :, kv], preferred_element_type=jnp.float32
        ).astype(jnp.bfloat16)


def local_heads(query_states, key_states, value_states):
    prompts_here, length, columns = query_states.shape
    head_count = columns // HD
    group = HEADS // KV
    kv_count = max(1, head_count // group)
    first = lax.axis_index("mp") * head_count // group
    keys = lax.dynamic_slice_in_dim(key_states, first * HD, kv_count * HD, axis=2)
    values = lax.dynamic_slice_in_dim(value_states, first * HD, kv_count * HD, axis=2)
    spec = lambda width: pl.BlockSpec((1, length, width), lambda i: (i, 0, 0))
    return pl.pallas_call(
        heads_kernel,
        grid=(prompts_here,),
        in_specs=[spec(columns), spec(kv_count * HD), spec(kv_count * HD)],
        out_specs=spec(columns),
        out_shape=jax.ShapeDtypeStruct((prompts_here, length, columns), jnp.bfloat16),
    )(query_states, keys, values)


def params(collective_id=None):
    return pltpu.CompilerParams(
        collective_id=collective_id,
        has_side_effects=collective_id is not None,
        vmem_limit_bytes=40 * 2**20,
    )


def swap_kernel(perm_ref, chosen_ref, rows_ref, o_ref):
    chosen = chosen_ref[...] > 0
    for prompt in range(rows_ref.shape[0]):
        own = rows_ref[prompt].astype(jnp.float32)
        other = rows_ref[perm_ref[prompt]].astype(jnp.float32)
        o_ref[prompt] = jnp.where(chosen, other, own).astype(jnp.bfloat16)


def swap(prompt_perm, chosen, rows):
    vmem = pl.BlockSpec(memory_space=pltpu.VMEM)
    return pl.pallas_call(
        swap_kernel,
        in_specs=[pl.BlockSpec(memory_space=pltpu.SMEM), vmem, vmem],
        out_specs=vmem,
        out_shape=jax.ShapeDtypeStruct(rows.shape, rows.dtype),
        compiler_params=params(),
    )(prompt_perm, chosen, rows)


def place(devices):
    me = lax.axis_index("batch")
    core = lax.rem(me, 2)
    return devices // 2, lax.div(me, 2), core, me + 1 - 2 * core


def greet(chips, chip, core, mate):
    barrier = pltpu.get_barrier_semaphore()
    for peer in [mate] + [2 * lax.rem(chip + k, chips) + core for k in range(1, chips)]:
        pl.semaphore_signal(
            barrier, inc=1, device_id={"batch": peer}, device_id_type=pl.DeviceIdType.MESH
        )
    pl.semaphore_wait(barrier, chips)


def send(src, dst, send_sem, recv_sem, peer):
    return pltpu.make_async_remote_copy(
        src_ref=src,
        dst_ref=dst,
        send_sem=send_sem,
        recv_sem=recv_sem,
        device_id={"batch": peer},
        device_id_type=pl.DeviceIdType.MESH,
    )


def scatter_kernel(x_ref, o_ref, near, part, far, send_near, recv_near, send_far, recv_far):
    chips, chip, core, mate = place(x_ref.shape[0])
    greet(chips, chip, core, mate)
    owner = [lax.rem(chip + k, chips) for k in range(chips)]
    order = list(range(1, chips)) + [0]
    to_mate = {}
    for k in order:
        to_mate[k] = send(
            x_ref.at[2 * owner[k] + 1 - core], near.at[k], send_near.at[k], recv_near.at[k], mate
        )
        to_mate[k].start()
    away = []
    for k in range(1, chips):
        to_mate[k].wait_recv()
        target = 2 * owner[k] + core
        part[k - 1] = (x_ref[target].astype(jnp.float32) + near[k].astype(jnp.float32)).astype(
            jnp.bfloat16
        )
        copy = send(
            part.at[k - 1], far.at[k - 1], send_far.at[k - 1], recv_far.at[k - 1], target
        )
        copy.start()
        away.append(copy)
    to_mate[0].wait_recv()
    total = x_ref[2 * chip + core].astype(jnp.float32) + near[0].astype(jnp.float32)
    for k in range(1, chips):
        away[k - 1].wait_recv()
        total = total + far[k - 1].astype(jnp.float32)
    o_ref[...] = total.astype(jnp.bfloat16)
    for k in order:
        to_mate[k].wait_send()
    for copy in away:
        copy.wait_send()


def scatter_sum(x):
    devices, rows, columns = x.shape
    chips = devices // 2
    vmem = pl.BlockSpec(memory_space=pltpu.VMEM)
    return pl.pallas_call(
        scatter_kernel,
        in_specs=[vmem],
        out_specs=vmem,
        out_shape=jax.ShapeDtypeStruct((rows, columns), jnp.bfloat16),
        scratch_shapes=[
            pltpu.VMEM((chips, rows, columns), jnp.bfloat16),
            pltpu.VMEM((chips - 1, rows, columns), jnp.bfloat16),
            pltpu.VMEM((chips - 1, rows, columns), jnp.bfloat16),
            pltpu.SemaphoreType.DMA((chips,)),
            pltpu.SemaphoreType.DMA((chips,)),
            pltpu.SemaphoreType.DMA((chips - 1,)),
            pltpu.SemaphoreType.DMA((chips - 1,)),
        ],
        compiler_params=params(1),
    )(x)


def gather_kernel(devices, x_ref, q_ref, ox_ref, oq_ref, send_far, recv_far, send_near, recv_near):
    chips, chip, core, mate = place(devices)
    me = 2 * chip + core
    greet(chips, chip, core, mate)
    pairs = ((x_ref, ox_ref), (q_ref, oq_ref))
    sent = []
    for k in range(1, chips):
        target = 2 * lax.rem(chip + k, chips) + core
        for i, (src, dst) in enumerate(pairs):
            copy = send(src, dst.at[me], send_far.at[k - 1, i], recv_far.at[k - 1, i], target)
            copy.start()
            sent.append(copy)
    for i, (src, dst) in enumerate(pairs):
        copy = send(src, dst.at[me], send_near.at[0, i], recv_near.at[0, i], mate)
        copy.start()
        sent.append(copy)
    ox_ref[me] = x_ref[...]
    oq_ref[me] = q_ref[...]
    for k in range(1, chips):
        source = 2 * lax.rem(chip + chips - k, chips) + core
        for i, (src, dst) in enumerate(pairs):
            send(
                src, dst.at[source], send_far.at[k - 1, i], recv_far.at[k - 1, i], mate
            ).wait_recv()
            copy = send(
                dst.at[source], dst.at[source], send_near.at[k, i], recv_near.at[k, i], mate
            )
            copy.start()
            sent.append(copy)
    for k in range(chips):
        source = 2 * lax.rem(chip + chips - k, chips) + 1 - core
        for i, (src, dst) in enumerate(pairs):
            send(src, dst.at[source], send_near.at[k, i], recv_near.at[k, i], mate).wait_recv()
    for copy in sent:
        copy.wait_send()


def gather_rows(x, squares):
    devices = lax.axis_size("batch")
    chips = devices // 2
    vmem = pl.BlockSpec(memory_space=pltpu.VMEM)
    return pl.pallas_call(
        functools.partial(gather_kernel, devices),
        in_specs=[vmem, vmem],
        out_specs=[vmem, vmem],
        out_shape=[
            jax.ShapeDtypeStruct((devices, *x.shape), x.dtype),
            jax.ShapeDtypeStruct((devices, *squares.shape), squares.dtype),
        ],
        scratch_shapes=[
            pltpu.SemaphoreType.DMA((chips - 1, 2)),
            pltpu.SemaphoreType.DMA((chips - 1, 2)),
            pltpu.SemaphoreType.DMA((chips, 2)),
            pltpu.SemaphoreType.DMA((chips, 2)),
        ],
        compiler_params=params(2),
    )(x, squares)


def body(
    residual,
    query_states,
    key_states,
    value_states,
    prompt_perm,
    ablated_heads,
    out_weight,
    rms_gain,
    gate_weight,
    up_weight,
    down_weight,
):
    prompts_here, length, model_cols = residual.shape
    local_rows = prompts_here * length
    batches = lax.axis_size("batch")
    head_block = local_heads(query_states, key_states, value_states)
    all_heads = lax.all_gather(head_block, "mp", axis=2, tiled=True)
    owned_cols = out_weight.shape[0]
    by_owner = all_heads.reshape(local_rows, batches, owned_cols).transpose(1, 0, 2)
    mine = lax.all_to_all(by_owner, "batch", 0, 0, tiled=True)
    prompts = batches * prompts_here
    mine = mine.reshape(prompts, length, owned_cols)
    head_of_col = (lax.axis_index("batch") * owned_cols + jnp.arange(owned_cols)) // HD
    chosen = jnp.any(head_of_col[:, None] == ablated_heads[None, :], axis=1)
    chosen = jnp.where(chosen, 1.0, 0.0).astype(jnp.float32)[None, :]
    ablated = swap(prompt_perm, chosen, mine).reshape(prompts * length, owned_cols)
    attn_part = jnp.dot(ablated, out_weight, preferred_element_type=jnp.float32)
    attn_out = scatter_sum(attn_part.astype(jnp.bfloat16).reshape(batches, local_rows, model_cols))
    hidden_state = residual.reshape(local_rows, model_cols).astype(jnp.float32) + attn_out.astype(
        jnp.float32
    )
    squares = jnp.sum(hidden_state * hidden_state, axis=1, keepdims=True)
    scaled = (hidden_state * rms_gain[None, :]).astype(jnp.bfloat16)
    block_rows, square_rows = gather_rows(scaled, jnp.broadcast_to(squares, (local_rows, 128)))
    block_rows = block_rows.reshape(batches * local_rows, model_cols)
    gate_part = jnp.dot(block_rows, gate_weight, preferred_element_type=jnp.float32)
    up_part = jnp.dot(block_rows, up_weight, preferred_element_type=jnp.float32)
    gate = lax.psum_scatter(
        gate_part.astype(jnp.bfloat16), "mp", scatter_dimension=0, tiled=True
    ).astype(jnp.float32)
    up = lax.psum_scatter(
        up_part.astype(jnp.bfloat16), "mp", scatter_dimension=0, tiled=True
    ).astype(jnp.float32)
    share = gate.shape[0]
    squares = lax.psum(square_rows[:, :, 0].reshape(batches * local_rows), "mp")
    squares = lax.dynamic_slice_in_dim(squares, lax.axis_index("mp") * share, share)
    inverse = lax.rsqrt(squares / D + 1e-05)[:, None]
    hidden = (jax.nn.silu(gate * inverse) * (up * inverse)).astype(jnp.bfloat16)
    hidden = lax.all_gather(hidden, "mp", axis=0, tiled=True)
    mlp_part = jnp.dot(hidden, down_weight, preferred_element_type=jnp.float32)
    mlp_float = scatter_sum(mlp_part.astype(jnp.bfloat16).reshape(batches, local_rows, model_cols))
    return (
        attn_out.reshape(prompts_here, length, model_cols),
        mlp_float.reshape(prompts_here, length, model_cols),
    )


def solution(mesh):
    placed = (
        P("batch", None, "mp"),
        P("batch", None, "mp"),
        P("batch", None, None),
        P("batch", None, None),
        P(),
        P(),
        P("batch", "mp"),
        P("mp"),
        P("mp", "batch"),
        P("mp", "batch"),
        P("batch", "mp"),
    )
    return jax.shard_map(
        body,
        mesh=mesh,
        in_specs=placed,
        out_specs=(P("batch", None, "mp"), P("batch", None, "mp")),
        check_vma=False,
    )
```

```python
import functools
import functools
import math

import jax
import jax.numpy as jnp
from jax import lax
from jax.experimental import pallas as pl
from jax.experimental.pallas import tpu as pltpu
from jax.sharding import PartitionSpec as P

D = 8192
HEADS = 32
KV = 4
HD = 128
ABLATED = 8


def heads_kernel(q_ref, k_ref, v_ref, o_ref):
    length = q_ref.shape[1]
    rows = lax.broadcasted_iota(jnp.int32, (length, length), 0)
    cols = lax.broadcasted_iota(jnp.int32, (length, length), 1)
    causal = rows >= cols
    for head in range(q_ref.shape[2] // HD):
        at = slice(head * HD, (head + 1) * HD)
        kv = slice(head * k_ref.shape[2] * HD // q_ref.shape[2] // HD * HD, None)
        kv = slice(kv.start, kv.start + HD)
        scores = lax.dot_general(
            q_ref[0, :, at],
            k_ref[0, :, kv],
            (((1,), (1,)), ((), ())),
            preferred_element_type=jnp.float32,
        ) / math.sqrt(HD)
        scores = jnp.where(causal, scores, -1e30)
        highest = jnp.max(scores, axis=-1, keepdims=True)
        weights = jnp.exp(scores - highest)
        probability = (weights / jnp.sum(weights, axis=-1, keepdims=True)).astype(jnp.bfloat16)
        o_ref[0, :, at] = jnp.dot(
            probability, v_ref[0, :, kv], preferred_element_type=jnp.float32
        ).astype(jnp.bfloat16)


def local_heads(query_states, key_states, value_states):
    prompts_here, length, columns = query_states.shape
    head_count = columns // HD
    group = HEADS // KV
    kv_count = max(1, head_count // group)
    first = lax.axis_index("mp") * head_count // group
    keys = lax.dynamic_slice_in_dim(key_states, first * HD, kv_count * HD, axis=2)
    values = lax.dynamic_slice_in_dim(value_states, first * HD, kv_count * HD, axis=2)
    spec = lambda width: pl.BlockSpec((1, length, width), lambda i: (i, 0, 0))
    return pl.pallas_call(
        heads_kernel,
        grid=(prompts_here,),
        in_specs=[spec(columns), spec(kv_count * HD), spec(kv_count * HD)],
        out_specs=spec(columns),
        out_shape=jax.ShapeDtypeStruct((prompts_here, length, columns), jnp.bfloat16),
    )(query_states, keys, values)


def params(collective_id=None):
    return pltpu.CompilerParams(
        collective_id=collective_id,
        has_side_effects=collective_id is not None,
        vmem_limit_bytes=40 * 2**20,
    )


def swap_kernel(perm_ref, chosen_ref, rows_ref, o_ref):
    chosen = chosen_ref[...] > 0
    for prompt in range(rows_ref.shape[0]):
        own = rows_ref[prompt].astype(jnp.float32)
        other = rows_ref[perm_ref[prompt]].astype(jnp.float32)
        o_ref[prompt] = jnp.where(chosen, other, own).astype(jnp.bfloat16)


def swap(prompt_perm, chosen, rows):
    vmem = pl.BlockSpec(memory_space=pltpu.VMEM)
    return pl.pallas_call(
        swap_kernel,
        in_specs=[pl.BlockSpec(memory_space=pltpu.SMEM), vmem, vmem],
        out_specs=vmem,
        out_shape=jax.ShapeDtypeStruct(rows.shape, rows.dtype),
        compiler_params=params(),
    )(prompt_perm, chosen, rows)


def place(devices):
    me = lax.axis_index("batch")
    core = lax.rem(me, 2)
    return devices // 2, lax.div(me, 2), core, me + 1 - 2 * core


def greet(chips, chip, core, mate):
    barrier = pltpu.get_barrier_semaphore()
    for peer in [mate] + [2 * lax.rem(chip + k, chips) + core for k in range(1, chips)]:
        pl.semaphore_signal(
            barrier, inc=1, device_id={"batch": peer}, device_id_type=pl.DeviceIdType.MESH
        )
    pl.semaphore_wait(barrier, chips)


def send(src, dst, send_sem, recv_sem, peer):
    return pltpu.make_async_remote_copy(
        src_ref=src,
        dst_ref=dst,
        send_sem=send_sem,
        recv_sem=recv_sem,
        device_id={"batch": peer},
        device_id_type=pl.DeviceIdType.MESH,
    )


def scatter_kernel(x_ref, o_ref, near, part, far, send_near, recv_near, send_far, recv_far):
    chips, chip, core, mate = place(x_ref.shape[0])
    greet(chips, chip, core, mate)
    owner = [lax.rem(chip + k, chips) for k in range(chips)]
    order = list(range(1, chips)) + [0]
    to_mate = {}
    for k in order:
        to_mate[k] = send(
            x_ref.at[2 * owner[k] + 1 - core], near.at[k], send_near.at[k], recv_near.at[k], mate
        )
        to_mate[k].start()
    away = []
    for k in range(1, chips):
        to_mate[k].wait_recv()
        target = 2 * owner[k] + core
        part[k - 1] = (x_ref[target].astype(jnp.float32) + near[k].astype(jnp.float32)).astype(
            jnp.bfloat16
        )
        copy = send(
            part.at[k - 1], far.at[k - 1], send_far.at[k - 1], recv_far.at[k - 1], target
        )
        copy.start()
        away.append(copy)
    to_mate[0].wait_recv()
    total = x_ref[2 * chip + core].astype(jnp.float32) + near[0].astype(jnp.float32)
    for k in range(1, chips):
        away[k - 1].wait_recv()
        total = total + far[k - 1].astype(jnp.float32)
    o_ref[...] = total.astype(jnp.bfloat16)
    for k in order:
        to_mate[k].wait_send()
    for copy in away:
        copy.wait_send()


def scatter_sum(x):
    devices, rows, columns = x.shape
    chips = devices // 2
    vmem = pl.BlockSpec(memory_space=pltpu.VMEM)
    return pl.pallas_call(
        scatter_kernel,
        in_specs=[vmem],
        out_specs=vmem,
        out_shape=jax.ShapeDtypeStruct((rows, columns), jnp.bfloat16),
        scratch_shapes=[
            pltpu.VMEM((chips, rows, columns), jnp.bfloat16),
            pltpu.VMEM((chips - 1, rows, columns), jnp.bfloat16),
            pltpu.VMEM((chips - 1, rows, columns), jnp.bfloat16),
            pltpu.SemaphoreType.DMA((chips,)),
            pltpu.SemaphoreType.DMA((chips,)),
            pltpu.SemaphoreType.DMA((chips - 1,)),
            pltpu.SemaphoreType.DMA((chips - 1,)),
        ],
        compiler_params=params(1),
    )(x)


def gather_kernel(devices, x_ref, q_ref, ox_ref, oq_ref, send_far, recv_far, send_near, recv_near):
    chips, chip, core, mate = place(devices)
    me = 2 * chip + core
    greet(chips, chip, core, mate)
    pairs = ((x_ref, ox_ref), (q_ref, oq_ref))
    sent = []
    for k in range(1, chips):
        target = 2 * lax.rem(chip + k, chips) + core
        for i, (src, dst) in enumerate(pairs):
            copy = send(src, dst.at[me], send_far.at[k - 1, i], recv_far.at[k - 1, i], target)
            copy.start()
            sent.append(copy)
    for i, (src, dst) in enumerate(pairs):
        copy = send(src, dst.at[me], send_near.at[0, i], recv_near.at[0, i], mate)
        copy.start()
        sent.append(copy)
    ox_ref[me] = x_ref[...]
    oq_ref[me] = q_ref[...]
    for k in range(1, chips):
        source = 2 * lax.rem(chip + chips - k, chips) + core
        for i, (src, dst) in enumerate(pairs):
            send(
                src, dst.at[source], send_far.at[k - 1, i], recv_far.at[k - 1, i], mate
            ).wait_recv()
            copy = send(
                dst.at[source], dst.at[source], send_near.at[k, i], recv_near.at[k, i], mate
            )
            copy.start()
            sent.append(copy)
    for k in range(chips):
        source = 2 * lax.rem(chip + chips - k, chips) + 1 - core
        for i, (src, dst) in enumerate(pairs):
            send(src, dst.at[source], send_near.at[k, i], recv_near.at[k, i], mate).wait_recv()
    for copy in sent:
        copy.wait_send()


def gather_rows(x, squares):
    devices = lax.axis_size("batch")
    chips = devices // 2
    vmem = pl.BlockSpec(memory_space=pltpu.VMEM)
    return pl.pallas_call(
        functools.partial(gather_kernel, devices),
        in_specs=[vmem, vmem],
        out_specs=[vmem, vmem],
        out_shape=[
            jax.ShapeDtypeStruct((devices, *x.shape), x.dtype),
            jax.ShapeDtypeStruct((devices, *squares.shape), squares.dtype),
        ],
        scratch_shapes=[
            pltpu.SemaphoreType.DMA((chips - 1, 2)),
            pltpu.SemaphoreType.DMA((chips - 1, 2)),
            pltpu.SemaphoreType.DMA((chips, 2)),
            pltpu.SemaphoreType.DMA((chips, 2)),
        ],
        compiler_params=params(2),
    )(x, squares)


def hidden_kernel(
    n, lag, x_ref, sq_ref, gate_ref, up_ref, o_ref, gate_buf, up_buf, own, got, squares,
    weight_sem, send_sum, recv_sum, send_hid, recv_hid, send_sq, recv_sq,
):
    m = lax.axis_index("mp")
    count, _, tokens, w = own.shape
    half = tokens // 2
    rows_of = (pl.ds(half, half), pl.ds(0, half))
    last_of = (n - 1, 0)
    pos_of = (m, n - 1 - m)
    way_of = (1, -1)

    def columns(c):
        return pl.ds(0, w) if count == 1 else pl.ds(pl.multiple_of(c * w, w), w)

    def fetch(c, slot):
        return [
            pltpu.make_async_copy(src.at[:, columns(c)], dst.at[slot], weight_sem.at[slot, i])
            for i, (src, dst) in enumerate(((gate_ref, gate_buf), (up_ref, up_buf)))
        ]

    def remote(src, dst, send_sem, recv_sem, peer):
        return pltpu.make_async_remote_copy(
            src_ref=src,
            dst_ref=dst,
            send_sem=send_sem,
            recv_sem=recv_sem,
            device_id={"mp": peer},
            device_id_type=pl.DeviceIdType.MESH,
        )

    def sum_copy(d, c, peer):
        return remote(
            own.at[c, :, rows_of[d], :],
            got.at[d, c],
            send_sum.at[d, c],
            recv_sum.at[d, c],
            peer,
        )

    def hid_copy(d, c, peer):
        block = o_ref.at[rows_of[d], columns(c)]
        return remote(block, block, send_hid.at[d, c], recv_hid.at[d, c], peer)

    def sq_copy(d, slot):
        return remote(
            sq_ref.at[rows_of[d], :],
            squares.at[slot],
            send_sq.at[d],
            recv_sq.at[slot],
            last_of[d],
        )

    for copy in fetch(0, 0):
        copy.start()
    barrier = pltpu.get_barrier_semaphore()
    for k in range(1, n):
        pl.semaphore_signal(
            barrier,
            inc=1,
            device_id={"mp": lax.rem(m + k, n)},
            device_id_type=pl.DeviceIdType.MESH,
        )
    pl.semaphore_wait(barrier, n - 1)
    for d in range(2):

        @pl.when(m != last_of[d])
        def _(d=d):
            sq_copy(d, m).start()

    def step(t, carry):
        @pl.when(t < count)
        def _():
            slot = lax.rem(t, 2)
            for copy in fetch(t, slot):
                copy.wait()

            @pl.when(t + 1 < count)
            def _():
                for copy in fetch(t + 1, 1 - slot):
                    copy.start()

            x = x_ref[...]
            if w % 128 == 0:
                both = jnp.concatenate([gate_buf[slot], up_buf[slot]], axis=1)
                made = jnp.dot(x, both, preferred_element_type=jnp.float32).astype(jnp.bfloat16)
                own[t, 0] = made[:, :w]
                own[t, 1] = made[:, w:]
            else:
                for i, buf in enumerate((gate_buf, up_buf)):
                    own[t, i] = jnp.dot(
                        x, buf[slot], preferred_element_type=jnp.float32
                    ).astype(jnp.bfloat16)

        for d in range(2):
            pos, rows, way = pos_of[d], rows_of[d], way_of[d]
            c = t - lag * pos
            here = (c >= 0) & (c < count)

            @pl.when(here & (pos == 0))
            def _(d=d, c=c, way=way):
                sum_copy(d, c, m + way).start()

            @pl.when(here & (pos > 0) & (pos < n - 1))
            def _(d=d, c=c, way=way, rows=rows):
                sum_copy(d, c, m - way).wait_recv()
                own[c, :, rows, :] = (
                    own[c, :, rows, :].astype(jnp.float32) + got[d, c].astype(jnp.float32)
                ).astype(jnp.bfloat16)
                sum_copy(d, c, m + way).start()

            @pl.when(here & (pos == n - 1))
            def _(d=d, c=c, way=way, rows=rows):
                @pl.when(c == 0)
                def _():
                    for k in range(1, n):
                        sq_copy(d, n - 1 - k if d == 0 else k).wait_recv()

                total = sq_ref[rows, :]
                for k in range(1, n):
                    total = total + squares[n - 1 - k if d == 0 else k]
                inverse = lax.rsqrt(total / D + 1e-05)[:, :1]
                sum_copy(d, c, m - way).wait_recv()
                summed = own[c, :, rows, :].astype(jnp.float32) + got[d, c].astype(jnp.float32)
                gate = summed[0] * inverse
                up = summed[1] * inverse
                o_ref[rows, columns(c)] = (gate / (1.0 + jnp.exp(-gate)) * up).astype(jnp.bfloat16)
                hid_copy(d, c, m - way).start()

            back = t - lag * (2 * (n - 1) - pos)

            @pl.when((back >= 0) & (back < count) & (pos < n - 1))
            def _(d=d, back=back, way=way, pos=pos):
                hid_copy(d, back, m + way).wait_recv()

                @pl.when(pos > 0)
                def _():
                    hid_copy(d, back, m - way).start()

        return carry

    lax.fori_loop(0, count + 2 * lag * (n - 1), step, 0)

    def finish(c, carry):
        for d in range(2):
            pos, way = pos_of[d], way_of[d]

            @pl.when(pos < n - 1)
            def _(d=d, way=way):
                sum_copy(d, c, m + way).wait_send()

            @pl.when(pos > 0)
            def _(d=d, way=way):
                hid_copy(d, c, m - way).wait_send()

        return carry

    lax.fori_loop(0, count, finish, 0)
    for d in range(2):

        @pl.when(m != last_of[d])
        def _(d=d):
            sq_copy(d, m).wait_send()


def hidden_rows(x, squares, gate_weight, up_weight):
    n = lax.axis_size("mp")
    tokens, depth = x.shape
    width = gate_weight.shape[1]
    w = 128 if width % 128 == 0 else width
    count = width // w
    vmem = pl.BlockSpec(memory_space=pltpu.VMEM)
    anywhere = pl.BlockSpec(memory_space=pl.ANY)
    dma = pltpu.SemaphoreType.DMA
    return pl.pallas_call(
        functools.partial(hidden_kernel, n, 2 if count > 1 else 1),
        in_specs=[vmem, vmem, anywhere, anywhere],
        out_specs=vmem,
        out_shape=jax.ShapeDtypeStruct((tokens, width), jnp.bfloat16),
        scratch_shapes=[
            pltpu.VMEM((2, depth, w), jnp.bfloat16),
            pltpu.VMEM((2, depth, w), jnp.bfloat16),
            pltpu.VMEM((count, 2, tokens, w), jnp.bfloat16),
            pltpu.VMEM((2, count, 2, tokens // 2, w), jnp.bfloat16),
            pltpu.VMEM((n, tokens // 2, 128), jnp.float32),
            dma((2, 2)),
            dma((2, count)),
            dma((2, count)),
            dma((2, count)),
            dma((2, count)),
            dma((2,)),
            dma((n,)),
        ],
        compiler_params=params(3),
    )(x, squares, gate_weight, up_weight)


def body(
    residual,
    query_states,
    key_states,
    value_states,
    prompt_perm,
    ablated_heads,
    out_weight,
    rms_gain,
    gate_weight,
    up_weight,
    down_weight,
):
    prompts_here, length, model_cols = residual.shape
    local_rows = prompts_here * length
    batches = lax.axis_size("batch")
    head_block = local_heads(query_states, key_states, value_states)
    all_heads = lax.all_gather(head_block, "mp", axis=2, tiled=True)
    owned_cols = out_weight.shape[0]
    by_owner = all_heads.reshape(local_rows, batches, owned_cols).transpose(1, 0, 2)
    mine = lax.all_to_all(by_owner, "batch", 0, 0, tiled=True)
    prompts = batches * prompts_here
    mine = mine.reshape(prompts, length, owned_cols)
    head_of_col = (lax.axis_index("batch") * owned_cols + jnp.arange(owned_cols)) // HD
    chosen = jnp.any(head_of_col[:, None] == ablated_heads[None, :], axis=1)
    chosen = jnp.where(chosen, 1.0, 0.0).astype(jnp.float32)[None, :]
    ablated = swap(prompt_perm, chosen, mine).reshape(prompts * length, owned_cols)
    attn_part = jnp.dot(ablated, out_weight, preferred_element_type=jnp.float32)
    attn_out = scatter_sum(attn_part.astype(jnp.bfloat16).reshape(batches, local_rows, model_cols))
    hidden_state = residual.reshape(local_rows, model_cols).astype(jnp.float32) + attn_out.astype(
        jnp.float32
    )
    squares = jnp.sum(hidden_state * hidden_state, axis=1, keepdims=True)
    scaled = (hidden_state * rms_gain[None, :]).astype(jnp.bfloat16)
    block_rows, square_rows = gather_rows(scaled, jnp.broadcast_to(squares, (local_rows, 128)))
    block_rows = block_rows.reshape(batches * local_rows, model_cols)
    square_rows = square_rows.reshape(batches * local_rows, 128)
    hidden = hidden_rows(block_rows, square_rows, gate_weight, up_weight)
    mlp_part = jnp.dot(hidden, down_weight, preferred_element_type=jnp.float32)
    mlp_float = scatter_sum(mlp_part.astype(jnp.bfloat16).reshape(batches, local_rows, model_cols))
    return (
        attn_out.reshape(prompts_here, length, model_cols),
        mlp_float.reshape(prompts_here, length, model_cols),
    )


def solution(mesh):
    placed = (
        P("batch", None, "mp"),
        P("batch", None, "mp"),
        P("batch", None, None),
        P("batch", None, None),
        P(),
        P(),
        P("batch", "mp"),
        P("mp"),
        P("mp", "batch"),
        P("mp", "batch"),
        P("batch", "mp"),
    )
    return jax.shard_map(
        body,
        mesh=mesh,
        in_specs=placed,
        out_specs=(P("batch", None, "mp"), P("batch", None, "mp")),
        check_vma=False,
    )
```

```python
import functools
import functools
import math

import jax
import jax.numpy as jnp
from jax import lax
from jax.experimental import pallas as pl
from jax.experimental.pallas import tpu as pltpu
from jax.sharding import PartitionSpec as P

D = 8192
HEADS = 32
KV = 4
HD = 128
ABLATED = 8


def heads_kernel(q_ref, k_ref, v_ref, o_ref, blocks, send_line, recv_line, send_owner, recv_owner):
    lines, owners, prompts, length, owned = blocks.shape
    devices = o_ref.shape[0]
    me, m = lax.axis_index("batch"), lax.axis_index("mp")
    barrier = pltpu.get_barrier_semaphore()
    for axis, at, size in (("mp", m, lines), ("batch", me, devices)):
        for k in range(1, size):
            pl.semaphore_signal(
                barrier,
                inc=1,
                device_id={axis: lax.rem(at + k, size)},
                device_id_type=pl.DeviceIdType.MESH,
            )
    rows = lax.broadcasted_iota(jnp.int32, (length, length), 0)
    cols = lax.broadcasted_iota(jnp.int32, (length, length), 1)
    causal = rows >= cols
    heads_here = q_ref.shape[2] // HD

    def line_copy(source, k, j, peer):
        block = blocks.at[source, j]
        return pltpu.make_async_remote_copy(
            src_ref=block,
            dst_ref=block,
            send_sem=send_line.at[k - 1, j],
            recv_sem=recv_line.at[k - 1, j],
            device_id={"mp": peer},
            device_id_type=pl.DeviceIdType.MESH,
        )

    def owner_copy(source, k, j, slot, peer):
        return pltpu.make_async_remote_copy(
            src_ref=blocks.at[source, j],
            dst_ref=o_ref.at[slot],
            send_sem=send_owner.at[k, j],
            recv_sem=recv_owner.at[slot],
            device_id={"batch": peer},
            device_id_type=pl.DeviceIdType.MESH,
        )

    def forward(source, k, j):
        owner = source * owners + j

        @pl.when(owner != me)
        def _():
            owner_copy(source, k, j, me, owner).start()

        @pl.when(owner == me)
        def _():
            o_ref[me] = blocks[source, j]

    for j in range(owners):
        for at in range(0, owned, HD):
            head = j * owned // HD + at // HD
            kv = lax.div(m * heads_here + head, HEADS // KV)
            kv = pl.ds(pl.multiple_of(kv * HD, HD), HD)
            for prompt in range(prompts):
                scores = lax.dot_general(
                    q_ref[prompt, :, head * HD : (head + 1) * HD],
                    k_ref[prompt, :, kv],
                    (((1,), (1,)), ((), ())),
                    preferred_element_type=jnp.float32,
                ) / math.sqrt(HD)
                scores = jnp.where(causal, scores, -1e30)
                highest = jnp.max(scores, axis=-1, keepdims=True)
                weights = jnp.exp(scores - highest)
                probability = weights / jnp.sum(weights, axis=-1, keepdims=True)
                blocks[m, j, prompt, :, at : at + HD] = jnp.dot(
                    probability.astype(jnp.bfloat16),
                    v_ref[prompt, :, kv],
                    preferred_element_type=jnp.float32,
                ).astype(jnp.bfloat16)
        if j == 0:
            pl.semaphore_wait(barrier, lines + devices - 2)
        for k in range(1, lines):
            line_copy(m, k, j, lax.rem(m + k, lines)).start()
        forward(m, 0, j)
    for k in range(1, lines):
        source = lax.rem(m + lines - k, lines)
        for j in range(owners):
            line_copy(source, k, j, source).wait_recv()
            forward(source, k, j)
    for k in range(1, devices):
        other = lax.rem(me + k, devices)
        owner_copy(m, 0, 0, other, other).wait_recv()
    for k in range(lines):
        source = lax.rem(m + lines - k, lines)
        for j in range(owners):
            if k > 0:
                line_copy(m, k, j, source).wait_send()

            @pl.when(source * owners + j != me)
            def _(source=source, k=k, j=j):
                owner_copy(source, k, j, me, source * owners + j).wait_send()


def owned_heads(query_states, key_states, value_states, owned):
    prompts, length, columns = query_states.shape
    devices, lines = lax.axis_size("batch"), lax.axis_size("mp")
    owners = columns // owned
    vmem = pl.BlockSpec(memory_space=pltpu.VMEM)
    dma = pltpu.SemaphoreType.DMA
    return pl.pallas_call(
        heads_kernel,
        in_specs=[vmem] * 3,
        out_specs=vmem,
        out_shape=jax.ShapeDtypeStruct((devices, prompts, length, owned), jnp.bfloat16),
        scratch_shapes=[
            pltpu.VMEM((lines, owners, prompts, length, owned), jnp.bfloat16),
            dma((lines - 1, owners)),
            dma((lines - 1, owners)),
            dma((lines, owners)),
            dma((devices,)),
        ],
        compiler_params=params(4),
    )(query_states, key_states, value_states)


def params(collective_id=None):
    return pltpu.CompilerParams(
        collective_id=collective_id,
        has_side_effects=collective_id is not None,
        vmem_limit_bytes=40 * 2**20,
    )


def swap_kernel(perm_ref, chosen_ref, rows_ref, o_ref):
    chosen = chosen_ref[...] > 0
    for prompt in range(rows_ref.shape[0]):
        own = rows_ref[prompt].astype(jnp.float32)
        other = rows_ref[perm_ref[prompt]].astype(jnp.float32)
        o_ref[prompt] = jnp.where(chosen, other, own).astype(jnp.bfloat16)


def swap(prompt_perm, chosen, rows):
    vmem = pl.BlockSpec(memory_space=pltpu.VMEM)
    return pl.pallas_call(
        swap_kernel,
        in_specs=[pl.BlockSpec(memory_space=pltpu.SMEM), vmem, vmem],
        out_specs=vmem,
        out_shape=jax.ShapeDtypeStruct(rows.shape, rows.dtype),
        compiler_params=params(),
    )(prompt_perm, chosen, rows)


def place(devices):
    me = lax.axis_index("batch")
    core = lax.rem(me, 2)
    return devices // 2, lax.div(me, 2), core, me + 1 - 2 * core


def greet(chips, chip, core, mate):
    barrier = pltpu.get_barrier_semaphore()
    for peer in [mate] + [2 * lax.rem(chip + k, chips) + core for k in range(1, chips)]:
        pl.semaphore_signal(
            barrier, inc=1, device_id={"batch": peer}, device_id_type=pl.DeviceIdType.MESH
        )
    pl.semaphore_wait(barrier, chips)


def send(src, dst, send_sem, recv_sem, peer):
    return pltpu.make_async_remote_copy(
        src_ref=src,
        dst_ref=dst,
        send_sem=send_sem,
        recv_sem=recv_sem,
        device_id={"batch": peer},
        device_id_type=pl.DeviceIdType.MESH,
    )


def scatter_kernel(x_ref, o_ref, near, part, far, send_near, recv_near, send_far, recv_far):
    chips, chip, core, mate = place(x_ref.shape[0])
    greet(chips, chip, core, mate)
    owner = [lax.rem(chip + k, chips) for k in range(chips)]
    order = list(range(1, chips)) + [0]
    to_mate = {}
    for k in order:
        to_mate[k] = send(
            x_ref.at[2 * owner[k] + 1 - core], near.at[k], send_near.at[k], recv_near.at[k], mate
        )
        to_mate[k].start()
    away = []
    for k in range(1, chips):
        to_mate[k].wait_recv()
        target = 2 * owner[k] + core
        part[k - 1] = (x_ref[target].astype(jnp.float32) + near[k].astype(jnp.float32)).astype(
            jnp.bfloat16
        )
        copy = send(
            part.at[k - 1], far.at[k - 1], send_far.at[k - 1], recv_far.at[k - 1], target
        )
        copy.start()
        away.append(copy)
    to_mate[0].wait_recv()
    total = x_ref[2 * chip + core].astype(jnp.float32) + near[0].astype(jnp.float32)
    for k in range(1, chips):
        away[k - 1].wait_recv()
        total = total + far[k - 1].astype(jnp.float32)
    o_ref[...] = total.astype(jnp.bfloat16)
    for k in order:
        to_mate[k].wait_send()
    for copy in away:
        copy.wait_send()


def scatter_sum(x):
    devices, rows, columns = x.shape
    chips = devices // 2
    vmem = pl.BlockSpec(memory_space=pltpu.VMEM)
    return pl.pallas_call(
        scatter_kernel,
        in_specs=[vmem],
        out_specs=vmem,
        out_shape=jax.ShapeDtypeStruct((rows, columns), jnp.bfloat16),
        scratch_shapes=[
            pltpu.VMEM((chips, rows, columns), jnp.bfloat16),
            pltpu.VMEM((chips - 1, rows, columns), jnp.bfloat16),
            pltpu.VMEM((chips - 1, rows, columns), jnp.bfloat16),
            pltpu.SemaphoreType.DMA((chips,)),
            pltpu.SemaphoreType.DMA((chips,)),
            pltpu.SemaphoreType.DMA((chips - 1,)),
            pltpu.SemaphoreType.DMA((chips - 1,)),
        ],
        compiler_params=params(1),
    )(x)


def gather_kernel(devices, x_ref, q_ref, ox_ref, oq_ref, send_far, recv_far, send_near, recv_near):
    chips, chip, core, mate = place(devices)
    me = 2 * chip + core
    greet(chips, chip, core, mate)
    pairs = ((x_ref, ox_ref), (q_ref, oq_ref))
    sent = []
    for k in range(1, chips):
        target = 2 * lax.rem(chip + k, chips) + core
        for i, (src, dst) in enumerate(pairs):
            copy = send(src, dst.at[me], send_far.at[k - 1, i], recv_far.at[k - 1, i], target)
            copy.start()
            sent.append(copy)
    for i, (src, dst) in enumerate(pairs):
        copy = send(src, dst.at[me], send_near.at[0, i], recv_near.at[0, i], mate)
        copy.start()
        sent.append(copy)
    ox_ref[me] = x_ref[...]
    oq_ref[me] = q_ref[...]
    for k in range(1, chips):
        source = 2 * lax.rem(chip + chips - k, chips) + core
        for i, (src, dst) in enumerate(pairs):
            send(
                src, dst.at[source], send_far.at[k - 1, i], recv_far.at[k - 1, i], mate
            ).wait_recv()
            copy = send(
                dst.at[source], dst.at[source], send_near.at[k, i], recv_near.at[k, i], mate
            )
            copy.start()
            sent.append(copy)
    for k in range(chips):
        source = 2 * lax.rem(chip + chips - k, chips) + 1 - core
        for i, (src, dst) in enumerate(pairs):
            send(src, dst.at[source], send_near.at[k, i], recv_near.at[k, i], mate).wait_recv()
    for copy in sent:
        copy.wait_send()


def gather_rows(x, squares):
    devices = lax.axis_size("batch")
    chips = devices // 2
    vmem = pl.BlockSpec(memory_space=pltpu.VMEM)
    return pl.pallas_call(
        functools.partial(gather_kernel, devices),
        in_specs=[vmem, vmem],
        out_specs=[vmem, vmem],
        out_shape=[
            jax.ShapeDtypeStruct((devices, *x.shape), x.dtype),
            jax.ShapeDtypeStruct((devices, *squares.shape), squares.dtype),
        ],
        scratch_shapes=[
            pltpu.SemaphoreType.DMA((chips - 1, 2)),
            pltpu.SemaphoreType.DMA((chips - 1, 2)),
            pltpu.SemaphoreType.DMA((chips, 2)),
            pltpu.SemaphoreType.DMA((chips, 2)),
        ],
        compiler_params=params(2),
    )(x, squares)


def hidden_kernel(
    n, lag, x_ref, sq_ref, gate_ref, up_ref, o_ref, gate_buf, up_buf, own, got, squares,
    weight_sem, send_sum, recv_sum, send_hid, recv_hid, send_sq, recv_sq,
):
    m = lax.axis_index("mp")
    count, _, tokens, w = own.shape
    half = tokens // 2
    rows_of = (pl.ds(half, half), pl.ds(0, half))
    last_of = (n - 1, 0)
    pos_of = (m, n - 1 - m)
    way_of = (1, -1)

    def columns(c):
        return pl.ds(0, w) if count == 1 else pl.ds(pl.multiple_of(c * w, w), w)

    def fetch(c, slot):
        return [
            pltpu.make_async_copy(src.at[:, columns(c)], dst.at[slot], weight_sem.at[slot, i])
            for i, (src, dst) in enumerate(((gate_ref, gate_buf), (up_ref, up_buf)))
        ]

    def remote(src, dst, send_sem, recv_sem, peer):
        return pltpu.make_async_remote_copy(
            src_ref=src,
            dst_ref=dst,
            send_sem=send_sem,
            recv_sem=recv_sem,
            device_id={"mp": peer},
            device_id_type=pl.DeviceIdType.MESH,
        )

    def sum_copy(d, c, peer):
        return remote(
            own.at[c, :, rows_of[d], :],
            got.at[d, c],
            send_sum.at[d, c],
            recv_sum.at[d, c],
            peer,
        )

    def hid_copy(d, c, peer):
        block = o_ref.at[rows_of[d], columns(c)]
        return remote(block, block, send_hid.at[d, c], recv_hid.at[d, c], peer)

    def sq_copy(d, slot):
        return remote(
            sq_ref.at[rows_of[d], :],
            squares.at[slot],
            send_sq.at[d],
            recv_sq.at[slot],
            last_of[d],
        )

    for copy in fetch(0, 0):
        copy.start()
    barrier = pltpu.get_barrier_semaphore()
    for k in range(1, n):
        pl.semaphore_signal(
            barrier,
            inc=1,
            device_id={"mp": lax.rem(m + k, n)},
            device_id_type=pl.DeviceIdType.MESH,
        )
    pl.semaphore_wait(barrier, n - 1)
    for d in range(2):

        @pl.when(m != last_of[d])
        def _(d=d):
            sq_copy(d, m).start()

    def step(t, carry):
        @pl.when(t < count)
        def _():
            slot = lax.rem(t, 2)
            for copy in fetch(t, slot):
                copy.wait()

            @pl.when(t + 1 < count)
            def _():
                for copy in fetch(t + 1, 1 - slot):
                    copy.start()

            x = x_ref[...]
            if w % 128 == 0:
                both = jnp.concatenate([gate_buf[slot], up_buf[slot]], axis=1)
                made = jnp.dot(x, both, preferred_element_type=jnp.float32).astype(jnp.bfloat16)
                own[t, 0] = made[:, :w]
                own[t, 1] = made[:, w:]
            else:
                for i, buf in enumerate((gate_buf, up_buf)):
                    own[t, i] = jnp.dot(
                        x, buf[slot], preferred_element_type=jnp.float32
                    ).astype(jnp.bfloat16)

        for d in range(2):
            pos, rows, way = pos_of[d], rows_of[d], way_of[d]
            c = t - lag * pos
            here = (c >= 0) & (c < count)

            @pl.when(here & (pos == 0))
            def _(d=d, c=c, way=way):
                sum_copy(d, c, m + way).start()

            @pl.when(here & (pos > 0) & (pos < n - 1))
            def _(d=d, c=c, way=way, rows=rows):
                sum_copy(d, c, m - way).wait_recv()
                own[c, :, rows, :] = (
                    own[c, :, rows, :].astype(jnp.float32) + got[d, c].astype(jnp.float32)
                ).astype(jnp.bfloat16)
                sum_copy(d, c, m + way).start()

            @pl.when(here & (pos == n - 1))
            def _(d=d, c=c, way=way, rows=rows):
                @pl.when(c == 0)
                def _():
                    for k in range(1, n):
                        sq_copy(d, n - 1 - k if d == 0 else k).wait_recv()

                total = sq_ref[rows, :]
                for k in range(1, n):
                    total = total + squares[n - 1 - k if d == 0 else k]
                inverse = lax.rsqrt(total / D + 1e-05)[:, :1]
                sum_copy(d, c, m - way).wait_recv()
                summed = own[c, :, rows, :].astype(jnp.float32) + got[d, c].astype(jnp.float32)
                gate = summed[0] * inverse
                up = summed[1] * inverse
                o_ref[rows, columns(c)] = (gate / (1.0 + jnp.exp(-gate)) * up).astype(jnp.bfloat16)
                hid_copy(d, c, m - way).start()

            back = t - lag * (2 * (n - 1) - pos)

            @pl.when((back >= 0) & (back < count) & (pos < n - 1))
            def _(d=d, back=back, way=way, pos=pos):
                hid_copy(d, back, m + way).wait_recv()

                @pl.when(pos > 0)
                def _():
                    hid_copy(d, back, m - way).start()

        return carry

    lax.fori_loop(0, count + 2 * lag * (n - 1), step, 0)

    def finish(c, carry):
        for d in range(2):
            pos, way = pos_of[d], way_of[d]

            @pl.when(pos < n - 1)
            def _(d=d, way=way):
                sum_copy(d, c, m + way).wait_send()

            @pl.when(pos > 0)
            def _(d=d, way=way):
                hid_copy(d, c, m - way).wait_send()

        return carry

    lax.fori_loop(0, count, finish, 0)
    for d in range(2):

        @pl.when(m != last_of[d])
        def _(d=d):
            sq_copy(d, m).wait_send()


def hidden_rows(x, squares, gate_weight, up_weight):
    n = lax.axis_size("mp")
    tokens, depth = x.shape
    width = gate_weight.shape[1]
    w = 128 if width % 128 == 0 else width
    count = width // w
    vmem = pl.BlockSpec(memory_space=pltpu.VMEM)
    anywhere = pl.BlockSpec(memory_space=pl.ANY)
    dma = pltpu.SemaphoreType.DMA
    return pl.pallas_call(
        functools.partial(hidden_kernel, n, 2 if count > 1 else 1),
        in_specs=[vmem, vmem, anywhere, anywhere],
        out_specs=vmem,
        out_shape=jax.ShapeDtypeStruct((tokens, width), jnp.bfloat16),
        scratch_shapes=[
            pltpu.VMEM((2, depth, w), jnp.bfloat16),
            pltpu.VMEM((2, depth, w), jnp.bfloat16),
            pltpu.VMEM((count, 2, tokens, w), jnp.bfloat16),
            pltpu.VMEM((2, count, 2, tokens // 2, w), jnp.bfloat16),
            pltpu.VMEM((n, tokens // 2, 128), jnp.float32),
            dma((2, 2)),
            dma((2, count)),
            dma((2, count)),
            dma((2, count)),
            dma((2, count)),
            dma((2,)),
            dma((n,)),
        ],
        compiler_params=params(3),
    )(x, squares, gate_weight, up_weight)


def body(
    residual,
    query_states,
    key_states,
    value_states,
    prompt_perm,
    ablated_heads,
    out_weight,
    rms_gain,
    gate_weight,
    up_weight,
    down_weight,
):
    prompts_here, length, model_cols = residual.shape
    local_rows = prompts_here * length
    batches = lax.axis_size("batch")
    owned_cols = out_weight.shape[0]
    mine = owned_heads(query_states, key_states, value_states, owned_cols)
    prompts = batches * prompts_here
    mine = mine.reshape(prompts, length, owned_cols)
    head_of_col = (lax.axis_index("batch") * owned_cols + jnp.arange(owned_cols)) // HD
    chosen = jnp.any(head_of_col[:, None] == ablated_heads[None, :], axis=1)
    chosen = jnp.where(chosen, 1.0, 0.0).astype(jnp.float32)[None, :]
    ablated = swap(prompt_perm, chosen, mine).reshape(prompts * length, owned_cols)
    attn_part = jnp.dot(ablated, out_weight, preferred_element_type=jnp.float32)
    attn_out = scatter_sum(attn_part.astype(jnp.bfloat16).reshape(batches, local_rows, model_cols))
    hidden_state = residual.reshape(local_rows, model_cols).astype(jnp.float32) + attn_out.astype(
        jnp.float32
    )
    squares = jnp.sum(hidden_state * hidden_state, axis=1, keepdims=True)
    scaled = (hidden_state * rms_gain[None, :]).astype(jnp.bfloat16)
    block_rows, square_rows = gather_rows(scaled, jnp.broadcast_to(squares, (local_rows, 128)))
    block_rows = block_rows.reshape(batches * local_rows, model_cols)
    square_rows = square_rows.reshape(batches * local_rows, 128)
    hidden = hidden_rows(block_rows, square_rows, gate_weight, up_weight)
    mlp_part = jnp.dot(hidden, down_weight, preferred_element_type=jnp.float32)
    mlp_float = scatter_sum(mlp_part.astype(jnp.bfloat16).reshape(batches, local_rows, model_cols))
    return (
        attn_out.reshape(prompts_here, length, model_cols),
        mlp_float.reshape(prompts_here, length, model_cols),
    )


def solution(mesh):
    placed = (
        P("batch", None, "mp"),
        P("batch", None, "mp"),
        P("batch", None, None),
        P("batch", None, None),
        P(),
        P(),
        P("batch", "mp"),
        P("mp"),
        P("mp", "batch"),
        P("mp", "batch"),
        P("batch", "mp"),
    )
    return jax.shard_map(
        body,
        mesh=mesh,
        in_specs=placed,
        out_specs=(P("batch", None, "mp"), P("batch", None, "mp")),
        check_vma=False,
    )
```

```python
import functools
import functools
import math

import jax
import jax.numpy as jnp
from jax import lax
from jax.experimental import pallas as pl
from jax.experimental.pallas import tpu as pltpu
from jax.sharding import PartitionSpec as P

D = 8192
HEADS = 32
KV = 4
HD = 128
ABLATED = 8


def heads_kernel(q_ref, k_ref, v_ref, o_ref, blocks, send_line, recv_line, send_owner, recv_owner):
    lines, owners, prompts, length, owned = blocks.shape
    devices = o_ref.shape[0]
    me, m = lax.axis_index("batch"), lax.axis_index("mp")
    barrier = pltpu.get_barrier_semaphore()
    for axis, at, size in (("mp", m, lines), ("batch", me, devices)):
        for k in range(1, size):
            pl.semaphore_signal(
                barrier,
                inc=1,
                device_id={axis: lax.rem(at + k, size)},
                device_id_type=pl.DeviceIdType.MESH,
            )
    rows = lax.broadcasted_iota(jnp.int32, (length, length), 0)
    cols = lax.broadcasted_iota(jnp.int32, (length, length), 1)
    causal = rows >= cols
    heads_here = q_ref.shape[2] // HD

    def line_copy(source, k, j, peer):
        block = blocks.at[source, j]
        return pltpu.make_async_remote_copy(
            src_ref=block,
            dst_ref=block,
            send_sem=send_line.at[k - 1, j],
            recv_sem=recv_line.at[k - 1, j],
            device_id={"mp": peer},
            device_id_type=pl.DeviceIdType.MESH,
        )

    def owner_copy(source, k, j, slot, peer):
        return pltpu.make_async_remote_copy(
            src_ref=blocks.at[source, j],
            dst_ref=o_ref.at[slot],
            send_sem=send_owner.at[k, j],
            recv_sem=recv_owner.at[slot],
            device_id={"batch": peer},
            device_id_type=pl.DeviceIdType.MESH,
        )

    def forward(source, k, j):
        owner = source * owners + j

        @pl.when(owner != me)
        def _():
            owner_copy(source, k, j, me, owner).start()

        @pl.when(owner == me)
        def _():
            o_ref[me] = blocks[source, j]

    for j in range(owners):
        for at in range(0, owned, HD):
            head = j * owned // HD + at // HD
            kv = lax.div(m * heads_here + head, HEADS // KV)
            kv = pl.ds(pl.multiple_of(kv * HD, HD), HD)
            for prompt in range(prompts):
                scores = lax.dot_general(
                    q_ref[prompt, :, head * HD : (head + 1) * HD],
                    k_ref[prompt, :, kv],
                    (((1,), (1,)), ((), ())),
                    preferred_element_type=jnp.float32,
                ) / math.sqrt(HD)
                scores = jnp.where(causal, scores, -1e30)
                highest = jnp.max(scores, axis=-1, keepdims=True)
                weights = jnp.exp(scores - highest)
                probability = weights / jnp.sum(weights, axis=-1, keepdims=True)
                blocks[m, j, prompt, :, at : at + HD] = jnp.dot(
                    probability.astype(jnp.bfloat16),
                    v_ref[prompt, :, kv],
                    preferred_element_type=jnp.float32,
                ).astype(jnp.bfloat16)
        if j == 0:
            pl.semaphore_wait(barrier, lines + devices - 2)
        for k in range(1, lines):
            line_copy(m, k, j, lax.rem(m + k, lines)).start()
        forward(m, 0, j)
    for k in range(1, lines):
        source = lax.rem(m + lines - k, lines)
        for j in range(owners):
            line_copy(source, k, j, source).wait_recv()
            forward(source, k, j)
    for k in range(1, devices):
        other = lax.rem(me + k, devices)
        owner_copy(m, 0, 0, other, other).wait_recv()
    for k in range(lines):
        source = lax.rem(m + lines - k, lines)
        for j in range(owners):
            if k > 0:
                line_copy(m, k, j, source).wait_send()

            @pl.when(source * owners + j != me)
            def _(source=source, k=k, j=j):
                owner_copy(source, k, j, me, source * owners + j).wait_send()


def owned_heads(query_states, key_states, value_states, owned):
    prompts, length, columns = query_states.shape
    devices, lines = lax.axis_size("batch"), lax.axis_size("mp")
    owners = columns // owned
    vmem = pl.BlockSpec(memory_space=pltpu.VMEM)
    dma = pltpu.SemaphoreType.DMA
    return pl.pallas_call(
        heads_kernel,
        in_specs=[vmem] * 3,
        out_specs=vmem,
        out_shape=jax.ShapeDtypeStruct((devices, prompts, length, owned), jnp.bfloat16),
        scratch_shapes=[
            pltpu.VMEM((lines, owners, prompts, length, owned), jnp.bfloat16),
            dma((lines - 1, owners)),
            dma((lines - 1, owners)),
            dma((lines, owners)),
            dma((devices,)),
        ],
        compiler_params=params(4),
    )(query_states, key_states, value_states)


def params(collective_id=None):
    return pltpu.CompilerParams(
        collective_id=collective_id,
        has_side_effects=collective_id is not None,
        vmem_limit_bytes=40 * 2**20,
    )


def swap_kernel(perm_ref, chosen_ref, rows_ref, o_ref):
    chosen = chosen_ref[...] > 0
    for prompt in range(rows_ref.shape[0]):
        own = rows_ref[prompt].astype(jnp.float32)
        other = rows_ref[perm_ref[prompt]].astype(jnp.float32)
        o_ref[prompt] = jnp.where(chosen, other, own).astype(jnp.bfloat16)


def swap(prompt_perm, chosen, rows):
    vmem = pl.BlockSpec(memory_space=pltpu.VMEM)
    return pl.pallas_call(
        swap_kernel,
        in_specs=[pl.BlockSpec(memory_space=pltpu.SMEM), vmem, vmem],
        out_specs=vmem,
        out_shape=jax.ShapeDtypeStruct(rows.shape, rows.dtype),
        compiler_params=params(),
    )(prompt_perm, chosen, rows)


def place(devices):
    me = lax.axis_index("batch")
    core = lax.rem(me, 2)
    return devices // 2, lax.div(me, 2), core, me + 1 - 2 * core


def greet(chips, chip, core, mate):
    barrier = pltpu.get_barrier_semaphore()
    for peer in [mate] + [2 * lax.rem(chip + k, chips) + core for k in range(1, chips)]:
        pl.semaphore_signal(
            barrier, inc=1, device_id={"batch": peer}, device_id_type=pl.DeviceIdType.MESH
        )
    pl.semaphore_wait(barrier, chips)


def send(src, dst, send_sem, recv_sem, peer):
    return pltpu.make_async_remote_copy(
        src_ref=src,
        dst_ref=dst,
        send_sem=send_sem,
        recv_sem=recv_sem,
        device_id={"batch": peer},
        device_id_type=pl.DeviceIdType.MESH,
    )


def scatter_kernel(x_ref, o_ref, near, part, far, send_near, recv_near, send_far, recv_far):
    chips, chip, core, mate = place(x_ref.shape[0])
    greet(chips, chip, core, mate)
    owner = [lax.rem(chip + k, chips) for k in range(chips)]
    rows = x_ref.shape[1]
    pieces = send_near.shape[1]
    piece = rows // pieces
    order = [(k, i) for k in (*range(1, chips), 0) for i in range(pieces)]
    to_mate = {}
    for k, i in order:
        at = pl.ds(i * piece, piece)
        to_mate[k, i] = send(
            x_ref.at[2 * owner[k] + 1 - core, at],
            near.at[k, at],
            send_near.at[k, i],
            recv_near.at[k, i],
            mate,
        )
        to_mate[k, i].start()
    away = {}
    for k, i in order:
        at = pl.ds(i * piece, piece)
        target = 2 * owner[k] + core
        to_mate[k, i].wait_recv()
        if k == 0:
            continue
        part[k - 1, at] = (
            x_ref[target, at].astype(jnp.float32) + near[k, at].astype(jnp.float32)
        ).astype(jnp.bfloat16)
        away[k, i] = send(
            part.at[k - 1, at],
            far.at[k - 1, at],
            send_far.at[k - 1, i],
            recv_far.at[k - 1, i],
            target,
        )
        away[k, i].start()
    total = x_ref[2 * chip + core].astype(jnp.float32) + near[0].astype(jnp.float32)
    for k in range(1, chips):
        for i in range(pieces):
            away[k, i].wait_recv()
        total = total + far[k - 1].astype(jnp.float32)
    o_ref[...] = total.astype(jnp.bfloat16)
    for copy in (*to_mate.values(), *away.values()):
        copy.wait_send()


def scatter_sum(x):
    devices, rows, columns = x.shape
    chips = devices // 2
    pieces = 2 if rows % 32 == 0 else 1
    vmem = pl.BlockSpec(memory_space=pltpu.VMEM)
    return pl.pallas_call(
        scatter_kernel,
        in_specs=[vmem],
        out_specs=vmem,
        out_shape=jax.ShapeDtypeStruct((rows, columns), jnp.bfloat16),
        scratch_shapes=[
            pltpu.VMEM((chips, rows, columns), jnp.bfloat16),
            pltpu.VMEM((chips - 1, rows, columns), jnp.bfloat16),
            pltpu.VMEM((chips - 1, rows, columns), jnp.bfloat16),
            pltpu.SemaphoreType.DMA((chips, pieces)),
            pltpu.SemaphoreType.DMA((chips, pieces)),
            pltpu.SemaphoreType.DMA((chips - 1, pieces)),
            pltpu.SemaphoreType.DMA((chips - 1, pieces)),
        ],
        compiler_params=params(1),
    )(x)


def gather_kernel(devices, x_ref, q_ref, ox_ref, oq_ref, send_far, recv_far, send_near, recv_near):
    chips, chip, core, mate = place(devices)
    me = 2 * chip + core
    greet(chips, chip, core, mate)
    pairs = ((x_ref, ox_ref), (q_ref, oq_ref))
    sent = []
    for k in range(1, chips):
        target = 2 * lax.rem(chip + k, chips) + core
        for i, (src, dst) in enumerate(pairs):
            copy = send(src, dst.at[me], send_far.at[k - 1, i], recv_far.at[k - 1, i], target)
            copy.start()
            sent.append(copy)
    for i, (src, dst) in enumerate(pairs):
        copy = send(src, dst.at[me], send_near.at[0, i], recv_near.at[0, i], mate)
        copy.start()
        sent.append(copy)
    ox_ref[me] = x_ref[...]
    oq_ref[me] = q_ref[...]
    for k in range(1, chips):
        source = 2 * lax.rem(chip + chips - k, chips) + core
        for i, (src, dst) in enumerate(pairs):
            send(
                src, dst.at[source], send_far.at[k - 1, i], recv_far.at[k - 1, i], mate
            ).wait_recv()
            copy = send(
                dst.at[source], dst.at[source], send_near.at[k, i], recv_near.at[k, i], mate
            )
            copy.start()
            sent.append(copy)
    for k in range(chips):
        source = 2 * lax.rem(chip + chips - k, chips) + 1 - core
        for i, (src, dst) in enumerate(pairs):
            send(src, dst.at[source], send_near.at[k, i], recv_near.at[k, i], mate).wait_recv()
    for copy in sent:
        copy.wait_send()


def gather_rows(x, squares):
    devices = lax.axis_size("batch")
    chips = devices // 2
    vmem = pl.BlockSpec(memory_space=pltpu.VMEM)
    return pl.pallas_call(
        functools.partial(gather_kernel, devices),
        in_specs=[vmem, vmem],
        out_specs=[vmem, vmem],
        out_shape=[
            jax.ShapeDtypeStruct((devices, *x.shape), x.dtype),
            jax.ShapeDtypeStruct((devices, *squares.shape), squares.dtype),
        ],
        scratch_shapes=[
            pltpu.SemaphoreType.DMA((chips - 1, 2)),
            pltpu.SemaphoreType.DMA((chips - 1, 2)),
            pltpu.SemaphoreType.DMA((chips, 2)),
            pltpu.SemaphoreType.DMA((chips, 2)),
        ],
        compiler_params=params(2),
    )(x, squares)


def hidden_kernel(
    n, lag, lag_back, x_ref, sq_ref, gate_ref, up_ref, o_ref, gate_buf, up_buf, own, got, squares,
    weight_sem, send_sum, recv_sum, send_hid, recv_hid, send_sq, recv_sq,
):
    m = lax.axis_index("mp")
    count, _, tokens, w = own.shape
    half = tokens // 2
    rows_of = (pl.ds(half, half), pl.ds(0, half))
    last_of = (n - 1, 0)
    pos_of = (m, n - 1 - m)
    way_of = (1, -1)

    def columns(c):
        return pl.ds(0, w) if count == 1 else pl.ds(pl.multiple_of(c * w, w), w)

    def fetch(c, slot):
        return [
            pltpu.make_async_copy(src.at[:, columns(c)], dst.at[slot], weight_sem.at[slot, i])
            for i, (src, dst) in enumerate(((gate_ref, gate_buf), (up_ref, up_buf)))
        ]

    def remote(src, dst, send_sem, recv_sem, peer):
        return pltpu.make_async_remote_copy(
            src_ref=src,
            dst_ref=dst,
            send_sem=send_sem,
            recv_sem=recv_sem,
            device_id={"mp": peer},
            device_id_type=pl.DeviceIdType.MESH,
        )

    def sum_copy(d, c, peer):
        return remote(
            own.at[c, :, rows_of[d], :],
            got.at[d, c],
            send_sum.at[d, c],
            recv_sum.at[d, c],
            peer,
        )

    def hid_copy(d, c, peer):
        block = o_ref.at[rows_of[d], columns(c)]
        return remote(block, block, send_hid.at[d, c], recv_hid.at[d, c], peer)

    def sq_copy(d, slot):
        return remote(
            sq_ref.at[rows_of[d], :],
            squares.at[slot],
            send_sq.at[d],
            recv_sq.at[slot],
            last_of[d],
        )

    for copy in fetch(0, 0):
        copy.start()
    barrier = pltpu.get_barrier_semaphore()
    for k in range(1, n):
        pl.semaphore_signal(
            barrier,
            inc=1,
            device_id={"mp": lax.rem(m + k, n)},
            device_id_type=pl.DeviceIdType.MESH,
        )
    pl.semaphore_wait(barrier, n - 1)
    for d in range(2):

        @pl.when(m != last_of[d])
        def _(d=d):
            sq_copy(d, m).start()

    def step(t, carry):
        @pl.when(t < count)
        def _():
            slot = lax.rem(t, 2)
            for copy in fetch(t, slot):
                copy.wait()

            @pl.when(t + 1 < count)
            def _():
                for copy in fetch(t + 1, 1 - slot):
                    copy.start()

            x = x_ref[...]
            if w % 128 == 0:
                both = jnp.concatenate([gate_buf[slot], up_buf[slot]], axis=1)
                made = jnp.dot(x, both, preferred_element_type=jnp.float32).astype(jnp.bfloat16)
                own[t, 0] = made[:, :w]
                own[t, 1] = made[:, w:]
            else:
                for i, buf in enumerate((gate_buf, up_buf)):
                    own[t, i] = jnp.dot(
                        x, buf[slot], preferred_element_type=jnp.float32
                    ).astype(jnp.bfloat16)

        for d in range(2):
            pos, rows, way = pos_of[d], rows_of[d], way_of[d]
            c = t - lag * pos
            here = (c >= 0) & (c < count)

            @pl.when(here & (pos == 0))
            def _(d=d, c=c, way=way):
                sum_copy(d, c, m + way).start()

            @pl.when(here & (pos > 0) & (pos < n - 1))
            def _(d=d, c=c, way=way, rows=rows):
                sum_copy(d, c, m - way).wait_recv()
                own[c, :, rows, :] = (
                    own[c, :, rows, :].astype(jnp.float32) + got[d, c].astype(jnp.float32)
                ).astype(jnp.bfloat16)
                sum_copy(d, c, m + way).start()

            @pl.when(here & (pos == n - 1))
            def _(d=d, c=c, way=way, rows=rows):
                @pl.when(c == 0)
                def _():
                    for k in range(1, n):
                        sq_copy(d, n - 1 - k if d == 0 else k).wait_recv()

                total = sq_ref[rows, :]
                for k in range(1, n):
                    total = total + squares[n - 1 - k if d == 0 else k]
                inverse = lax.rsqrt(total / D + 1e-05)[:, :1]
                sum_copy(d, c, m - way).wait_recv()
                summed = own[c, :, rows, :].astype(jnp.float32) + got[d, c].astype(jnp.float32)
                gate = summed[0] * inverse
                up = summed[1] * inverse
                o_ref[rows, columns(c)] = (gate / (1.0 + jnp.exp(-gate)) * up).astype(jnp.bfloat16)
                hid_copy(d, c, m - way).start()

            back = t - lag * (n - 1) - lag_back * (n - 1 - pos)

            @pl.when((back >= 0) & (back < count) & (pos < n - 1))
            def _(d=d, back=back, way=way, pos=pos):
                hid_copy(d, back, m + way).wait_recv()

                @pl.when(pos > 0)
                def _():
                    hid_copy(d, back, m - way).start()

        return carry

    lax.fori_loop(0, count + (lag + lag_back) * (n - 1), step, 0)

    def finish(c, carry):
        for d in range(2):
            pos, way = pos_of[d], way_of[d]

            @pl.when(pos < n - 1)
            def _(d=d, way=way):
                sum_copy(d, c, m + way).wait_send()

            @pl.when(pos > 0)
            def _(d=d, way=way):
                hid_copy(d, c, m - way).wait_send()

        return carry

    lax.fori_loop(0, count, finish, 0)
    for d in range(2):

        @pl.when(m != last_of[d])
        def _(d=d):
            sq_copy(d, m).wait_send()


def hidden_rows(x, squares, gate_weight, up_weight):
    n = lax.axis_size("mp")
    tokens, depth = x.shape
    width = gate_weight.shape[1]
    w = 128 if width % 128 == 0 else width
    count = width // w
    vmem = pl.BlockSpec(memory_space=pltpu.VMEM)
    anywhere = pl.BlockSpec(memory_space=pl.ANY)
    dma = pltpu.SemaphoreType.DMA
    return pl.pallas_call(
        functools.partial(hidden_kernel, n, 2 if count > 1 else 1, 1),
        in_specs=[vmem, vmem, anywhere, anywhere],
        out_specs=vmem,
        out_shape=jax.ShapeDtypeStruct((tokens, width), jnp.bfloat16),
        scratch_shapes=[
            pltpu.VMEM((2, depth, w), jnp.bfloat16),
            pltpu.VMEM((2, depth, w), jnp.bfloat16),
            pltpu.VMEM((count, 2, tokens, w), jnp.bfloat16),
            pltpu.VMEM((2, count, 2, tokens // 2, w), jnp.bfloat16),
            pltpu.VMEM((n, tokens // 2, 128), jnp.float32),
            dma((2, 2)),
            dma((2, count)),
            dma((2, count)),
            dma((2, count)),
            dma((2, count)),
            dma((2,)),
            dma((n,)),
        ],
        compiler_params=params(3),
    )(x, squares, gate_weight, up_weight)


def body(
    residual,
    query_states,
    key_states,
    value_states,
    prompt_perm,
    ablated_heads,
    out_weight,
    rms_gain,
    gate_weight,
    up_weight,
    down_weight,
):
    prompts_here, length, model_cols = residual.shape
    local_rows = prompts_here * length
    batches = lax.axis_size("batch")
    owned_cols = out_weight.shape[0]
    mine = owned_heads(query_states, key_states, value_states, owned_cols)
    prompts = batches * prompts_here
    mine = mine.reshape(prompts, length, owned_cols)
    head_of_col = (lax.axis_index("batch") * owned_cols + jnp.arange(owned_cols)) // HD
    chosen = jnp.any(head_of_col[:, None] == ablated_heads[None, :], axis=1)
    chosen = jnp.where(chosen, 1.0, 0.0).astype(jnp.float32)[None, :]
    ablated = swap(prompt_perm, chosen, mine).reshape(prompts * length, owned_cols)
    attn_part = jnp.dot(ablated, out_weight, preferred_element_type=jnp.float32)
    attn_out = scatter_sum(attn_part.astype(jnp.bfloat16).reshape(batches, local_rows, model_cols))
    hidden_state = residual.reshape(local_rows, model_cols).astype(jnp.float32) + attn_out.astype(
        jnp.float32
    )
    squares = jnp.sum(hidden_state * hidden_state, axis=1, keepdims=True)
    scaled = (hidden_state * rms_gain[None, :]).astype(jnp.bfloat16)
    block_rows, square_rows = gather_rows(scaled, jnp.broadcast_to(squares, (local_rows, 128)))
    block_rows = block_rows.reshape(batches * local_rows, model_cols)
    square_rows = square_rows.reshape(batches * local_rows, 128)
    hidden = hidden_rows(block_rows, square_rows, gate_weight, up_weight)
    mlp_part = jnp.dot(hidden, down_weight, preferred_element_type=jnp.float32)
    mlp_float = scatter_sum(mlp_part.astype(jnp.bfloat16).reshape(batches, local_rows, model_cols))
    return (
        attn_out.reshape(prompts_here, length, model_cols),
        mlp_float.reshape(prompts_here, length, model_cols),
    )


def solution(mesh):
    placed = (
        P("batch", None, "mp"),
        P("batch", None, "mp"),
        P("batch", None, None),
        P("batch", None, None),
        P(),
        P(),
        P("batch", "mp"),
        P("mp"),
        P("mp", "batch"),
        P("mp", "batch"),
        P("batch", "mp"),
    )
    return jax.shard_map(
        body,
        mesh=mesh,
        in_specs=placed,
        out_specs=(P("batch", None, "mp"), P("batch", None, "mp")),
        check_vma=False,
    )
```

```python
import functools
import functools
import math

import jax
import jax.numpy as jnp
from jax import lax
from jax.experimental import pallas as pl
from jax.experimental.pallas import tpu as pltpu
from jax.sharding import PartitionSpec as P

D = 8192
HEADS = 32
KV = 4
HD = 128
ABLATED = 8


def heads_kernel(q_ref, k_ref, v_ref, o_ref, blocks, send_line, recv_line, send_owner, recv_owner):
    lines, owners, prompts, length, owned = blocks.shape
    devices = o_ref.shape[0]
    me, m = lax.axis_index("batch"), lax.axis_index("mp")
    barrier = pltpu.get_barrier_semaphore()
    for axis, at, size in (("mp", m, lines), ("batch", me, devices)):
        for k in range(1, size):
            pl.semaphore_signal(
                barrier,
                inc=1,
                device_id={axis: lax.rem(at + k, size)},
                device_id_type=pl.DeviceIdType.MESH,
            )
    rows = lax.broadcasted_iota(jnp.int32, (length, length), 0)
    cols = lax.broadcasted_iota(jnp.int32, (length, length), 1)
    causal = rows >= cols
    heads_here = q_ref.shape[2] // HD

    def line_copy(source, k, j, peer):
        block = blocks.at[source, j]
        return pltpu.make_async_remote_copy(
            src_ref=block,
            dst_ref=block,
            send_sem=send_line.at[k - 1, j],
            recv_sem=recv_line.at[k - 1, j],
            device_id={"mp": peer},
            device_id_type=pl.DeviceIdType.MESH,
        )

    def owner_copy(source, k, j, slot, peer):
        return pltpu.make_async_remote_copy(
            src_ref=blocks.at[source, j],
            dst_ref=o_ref.at[slot],
            send_sem=send_owner.at[k, j],
            recv_sem=recv_owner.at[slot],
            device_id={"batch": peer},
            device_id_type=pl.DeviceIdType.MESH,
        )

    def forward(source, k, j):
        owner = source * owners + j

        @pl.when(owner != me)
        def _():
            owner_copy(source, k, j, me, owner).start()

        @pl.when(owner == me)
        def _():
            o_ref[me] = blocks[source, j]

    for j in range(owners):
        for at in range(0, owned, HD):
            head = j * owned // HD + at // HD
            kv = lax.div(m * heads_here + head, HEADS // KV)
            kv = pl.ds(pl.multiple_of(kv * HD, HD), HD)
            for prompt in range(prompts):
                scores = lax.dot_general(
                    q_ref[prompt, :, head * HD : (head + 1) * HD],
                    k_ref[prompt, :, kv],
                    (((1,), (1,)), ((), ())),
                    preferred_element_type=jnp.float32,
                ) / math.sqrt(HD)
                scores = jnp.where(causal, scores, -1e30)
                highest = jnp.max(scores, axis=-1, keepdims=True)
                weights = jnp.exp(scores - highest)
                probability = weights / jnp.sum(weights, axis=-1, keepdims=True)
                blocks[m, j, prompt, :, at : at + HD] = jnp.dot(
                    probability.astype(jnp.bfloat16),
                    v_ref[prompt, :, kv],
                    preferred_element_type=jnp.float32,
                ).astype(jnp.bfloat16)
        if j == 0:
            pl.semaphore_wait(barrier, lines + devices - 2)
        for k in range(1, lines):
            line_copy(m, k, j, lax.rem(m + k, lines)).start()
        forward(m, 0, j)
    for k in range(1, lines):
        source = lax.rem(m + lines - k, lines)
        for j in range(owners):
            line_copy(source, k, j, source).wait_recv()
            forward(source, k, j)
    for k in range(1, devices):
        other = lax.rem(me + k, devices)
        owner_copy(m, 0, 0, other, other).wait_recv()
    for k in range(lines):
        source = lax.rem(m + lines - k, lines)
        for j in range(owners):
            if k > 0:
                line_copy(m, k, j, source).wait_send()

            @pl.when(source * owners + j != me)
            def _(source=source, k=k, j=j):
                owner_copy(source, k, j, me, source * owners + j).wait_send()


def owned_heads(query_states, key_states, value_states, owned):
    prompts, length, columns = query_states.shape
    devices, lines = lax.axis_size("batch"), lax.axis_size("mp")
    owners = columns // owned
    vmem = pl.BlockSpec(memory_space=pltpu.VMEM)
    dma = pltpu.SemaphoreType.DMA
    return pl.pallas_call(
        heads_kernel,
        in_specs=[vmem] * 3,
        out_specs=vmem,
        out_shape=jax.ShapeDtypeStruct((devices, prompts, length, owned), jnp.bfloat16),
        scratch_shapes=[
            pltpu.VMEM((lines, owners, prompts, length, owned), jnp.bfloat16),
            dma((lines - 1, owners)),
            dma((lines - 1, owners)),
            dma((lines, owners)),
            dma((devices,)),
        ],
        compiler_params=params(4),
    )(query_states, key_states, value_states)


def params(collective_id=None):
    return pltpu.CompilerParams(
        collective_id=collective_id,
        has_side_effects=collective_id is not None,
        vmem_limit_bytes=40 * 2**20,
    )


def swap_kernel(perm_ref, chosen_ref, rows_ref, o_ref):
    chosen = chosen_ref[...] > 0
    for prompt in range(rows_ref.shape[0]):
        own = rows_ref[prompt].astype(jnp.float32)
        other = rows_ref[perm_ref[prompt]].astype(jnp.float32)
        o_ref[prompt] = jnp.where(chosen, other, own).astype(jnp.bfloat16)


def swap(prompt_perm, chosen, rows):
    vmem = pl.BlockSpec(memory_space=pltpu.VMEM)
    return pl.pallas_call(
        swap_kernel,
        in_specs=[pl.BlockSpec(memory_space=pltpu.SMEM), vmem, vmem],
        out_specs=vmem,
        out_shape=jax.ShapeDtypeStruct(rows.shape, rows.dtype),
        compiler_params=params(),
    )(prompt_perm, chosen, rows)


def place(devices):
    me = lax.axis_index("batch")
    core = lax.rem(me, 2)
    return devices // 2, lax.div(me, 2), core, me + 1 - 2 * core


def greet(chips, chip, core, mate):
    barrier = pltpu.get_barrier_semaphore()
    for peer in [mate] + [2 * lax.rem(chip + k, chips) + core for k in range(1, chips)]:
        pl.semaphore_signal(
            barrier, inc=1, device_id={"batch": peer}, device_id_type=pl.DeviceIdType.MESH
        )
    pl.semaphore_wait(barrier, chips)


def send(src, dst, send_sem, recv_sem, peer):
    return pltpu.make_async_remote_copy(
        src_ref=src,
        dst_ref=dst,
        send_sem=send_sem,
        recv_sem=recv_sem,
        device_id={"batch": peer},
        device_id_type=pl.DeviceIdType.MESH,
    )


def scatter_kernel(x_ref, o_ref, near, part, far, send_near, recv_near, send_far, recv_far):
    chips, chip, core, mate = place(x_ref.shape[0])
    greet(chips, chip, core, mate)
    owner = [lax.rem(chip + k, chips) for k in range(chips)]
    order = list(range(1, chips)) + [0]
    to_mate = {}
    for k in order:
        to_mate[k] = send(
            x_ref.at[2 * owner[k] + 1 - core], near.at[k], send_near.at[k], recv_near.at[k], mate
        )
        to_mate[k].start()
    away = []
    for k in range(1, chips):
        to_mate[k].wait_recv()
        target = 2 * owner[k] + core
        part[k - 1] = (x_ref[target].astype(jnp.float32) + near[k].astype(jnp.float32)).astype(
            jnp.bfloat16
        )
        copy = send(
            part.at[k - 1], far.at[k - 1], send_far.at[k - 1], recv_far.at[k - 1], target
        )
        copy.start()
        away.append(copy)
    to_mate[0].wait_recv()
    total = x_ref[2 * chip + core].astype(jnp.float32) + near[0].astype(jnp.float32)
    for k in range(1, chips):
        away[k - 1].wait_recv()
        total = total + far[k - 1].astype(jnp.float32)
    o_ref[...] = total.astype(jnp.bfloat16)
    for k in order:
        to_mate[k].wait_send()
    for copy in away:
        copy.wait_send()


def scatter_sum(x):
    devices, rows, columns = x.shape
    chips = devices // 2
    vmem = pl.BlockSpec(memory_space=pltpu.VMEM)
    return pl.pallas_call(
        scatter_kernel,
        in_specs=[vmem],
        out_specs=vmem,
        out_shape=jax.ShapeDtypeStruct((rows, columns), jnp.bfloat16),
        scratch_shapes=[
            pltpu.VMEM((chips, rows, columns), jnp.bfloat16),
            pltpu.VMEM((chips - 1, rows, columns), jnp.bfloat16),
            pltpu.VMEM((chips - 1, rows, columns), jnp.bfloat16),
            pltpu.SemaphoreType.DMA((chips,)),
            pltpu.SemaphoreType.DMA((chips,)),
            pltpu.SemaphoreType.DMA((chips - 1,)),
            pltpu.SemaphoreType.DMA((chips - 1,)),
        ],
        compiler_params=params(1),
    )(x)


def gather_kernel(devices, x_ref, q_ref, ox_ref, oq_ref, send_far, recv_far, send_near, recv_near):
    chips, chip, core, mate = place(devices)
    me = 2 * chip + core
    greet(chips, chip, core, mate)
    pairs = ((x_ref, ox_ref), (q_ref, oq_ref))
    sent = []
    for k in range(1, chips):
        target = 2 * lax.rem(chip + k, chips) + core
        for i, (src, dst) in enumerate(pairs):
            copy = send(src, dst.at[me], send_far.at[k - 1, i], recv_far.at[k - 1, i], target)
            copy.start()
            sent.append(copy)
    for i, (src, dst) in enumerate(pairs):
        copy = send(src, dst.at[me], send_near.at[0, i], recv_near.at[0, i], mate)
        copy.start()
        sent.append(copy)
    ox_ref[me] = x_ref[...]
    oq_ref[me] = q_ref[...]
    for k in range(1, chips):
        source = 2 * lax.rem(chip + chips - k, chips) + core
        for i, (src, dst) in enumerate(pairs):
            send(
                src, dst.at[source], send_far.at[k - 1, i], recv_far.at[k - 1, i], mate
            ).wait_recv()
            copy = send(
                dst.at[source], dst.at[source], send_near.at[k, i], recv_near.at[k, i], mate
            )
            copy.start()
            sent.append(copy)
    for k in range(chips):
        source = 2 * lax.rem(chip + chips - k, chips) + 1 - core
        for i, (src, dst) in enumerate(pairs):
            send(src, dst.at[source], send_near.at[k, i], recv_near.at[k, i], mate).wait_recv()
    for copy in sent:
        copy.wait_send()


def gather_rows(x, squares):
    devices = lax.axis_size("batch")
    chips = devices // 2
    vmem = pl.BlockSpec(memory_space=pltpu.VMEM)
    return pl.pallas_call(
        functools.partial(gather_kernel, devices),
        in_specs=[vmem, vmem],
        out_specs=[vmem, vmem],
        out_shape=[
            jax.ShapeDtypeStruct((devices, *x.shape), x.dtype),
            jax.ShapeDtypeStruct((devices, *squares.shape), squares.dtype),
        ],
        scratch_shapes=[
            pltpu.SemaphoreType.DMA((chips - 1, 2)),
            pltpu.SemaphoreType.DMA((chips - 1, 2)),
            pltpu.SemaphoreType.DMA((chips, 2)),
            pltpu.SemaphoreType.DMA((chips, 2)),
        ],
        compiler_params=params(2),
    )(x, squares)


def hidden_kernel(
    n, lag, x_ref, sq_ref, gate_ref, up_ref, o_ref, gate_buf, up_buf, own, got, squares,
    weight_sem, send_sum, recv_sum, send_hid, recv_hid, send_sq, recv_sq,
):
    m = lax.axis_index("mp")
    count, _, tokens, w = own.shape
    half = tokens // 2
    rows_of = (pl.ds(half, half), pl.ds(0, half))
    last_of = (n - 1, 0)
    pos_of = (m, n - 1 - m)
    way_of = (1, -1)

    def columns(c):
        return pl.ds(0, w) if count == 1 else pl.ds(pl.multiple_of(c * w, w), w)

    def fetch(c, slot):
        return [
            pltpu.make_async_copy(src.at[:, columns(c)], dst.at[slot], weight_sem.at[slot, i])
            for i, (src, dst) in enumerate(((gate_ref, gate_buf), (up_ref, up_buf)))
        ]

    def remote(src, dst, send_sem, recv_sem, peer):
        return pltpu.make_async_remote_copy(
            src_ref=src,
            dst_ref=dst,
            send_sem=send_sem,
            recv_sem=recv_sem,
            device_id={"mp": peer},
            device_id_type=pl.DeviceIdType.MESH,
        )

    def sum_copy(d, c, peer):
        return remote(
            own.at[c, :, rows_of[d], :],
            got.at[d, c],
            send_sum.at[d, c],
            recv_sum.at[d, c],
            peer,
        )

    def hid_copy(d, c, peer):
        block = o_ref.at[rows_of[d], columns(c)]
        return remote(block, block, send_hid.at[d, c], recv_hid.at[d, c], peer)

    def sq_copy(d, slot):
        return remote(
            sq_ref.at[rows_of[d], :],
            squares.at[slot],
            send_sq.at[d],
            recv_sq.at[slot],
            last_of[d],
        )

    for copy in fetch(0, 0):
        copy.start()
    barrier = pltpu.get_barrier_semaphore()
    for k in range(1, n):
        pl.semaphore_signal(
            barrier,
            inc=1,
            device_id={"mp": lax.rem(m + k, n)},
            device_id_type=pl.DeviceIdType.MESH,
        )
    pl.semaphore_wait(barrier, n - 1)
    for d in range(2):

        @pl.when(m != last_of[d])
        def _(d=d):
            sq_copy(d, m).start()

    def step(t, carry):
        @pl.when(t < count)
        def _():
            slot = lax.rem(t, 2)
            for copy in fetch(t, slot):
                copy.wait()

            @pl.when(t + 1 < count)
            def _():
                for copy in fetch(t + 1, 1 - slot):
                    copy.start()

            x = x_ref[...]
            if w % 128 == 0:
                both = jnp.concatenate([gate_buf[slot], up_buf[slot]], axis=1)
                made = jnp.dot(x, both, preferred_element_type=jnp.float32).astype(jnp.bfloat16)
                own[t, 0] = made[:, :w]
                own[t, 1] = made[:, w:]
            else:
                for i, buf in enumerate((gate_buf, up_buf)):
                    own[t, i] = jnp.dot(
                        x, buf[slot], preferred_element_type=jnp.float32
                    ).astype(jnp.bfloat16)

        for d in range(2):
            pos, rows, way = pos_of[d], rows_of[d], way_of[d]
            c = t - lag * pos
            here = (c >= 0) & (c < count)

            @pl.when(here & (pos == 0))
            def _(d=d, c=c, way=way):
                sum_copy(d, c, m + way).start()

            @pl.when(here & (pos > 0) & (pos < n - 1))
            def _(d=d, c=c, way=way, rows=rows):
                sum_copy(d, c, m - way).wait_recv()
                own[c, :, rows, :] = (
                    own[c, :, rows, :].astype(jnp.float32) + got[d, c].astype(jnp.float32)
                ).astype(jnp.bfloat16)
                sum_copy(d, c, m + way).start()

            @pl.when(here & (pos == n - 1))
            def _(d=d, c=c, way=way, rows=rows):
                @pl.when(c == 0)
                def _():
                    for k in range(1, n):
                        sq_copy(d, n - 1 - k if d == 0 else k).wait_recv()

                total = sq_ref[rows, :]
                for k in range(1, n):
                    total = total + squares[n - 1 - k if d == 0 else k]
                inverse = lax.rsqrt(total / D + 1e-05)[:, :1]
                sum_copy(d, c, m - way).wait_recv()
                summed = own[c, :, rows, :].astype(jnp.float32) + got[d, c].astype(jnp.float32)
                gate = summed[0] * inverse
                up = summed[1] * inverse
                o_ref[rows, columns(c)] = (gate / (1.0 + jnp.exp(-gate)) * up).astype(jnp.bfloat16)
                hid_copy(d, c, m - way).start()

            back = t - lag * (2 * (n - 1) - pos)

            @pl.when((back >= 0) & (back < count) & (pos < n - 1))
            def _(d=d, back=back, way=way, pos=pos):
                hid_copy(d, back, m + way).wait_recv()

                @pl.when(pos > 0)
                def _():
                    hid_copy(d, back, m - way).start()

        return carry

    lax.fori_loop(0, count + 2 * lag * (n - 1), step, 0)

    def finish(c, carry):
        for d in range(2):
            pos, way = pos_of[d], way_of[d]

            @pl.when(pos < n - 1)
            def _(d=d, way=way):
                sum_copy(d, c, m + way).wait_send()

            @pl.when(pos > 0)
            def _(d=d, way=way):
                hid_copy(d, c, m - way).wait_send()

        return carry

    lax.fori_loop(0, count, finish, 0)
    for d in range(2):

        @pl.when(m != last_of[d])
        def _(d=d):
            sq_copy(d, m).wait_send()


def hidden_rows(x, squares, gate_weight, up_weight):
    n = lax.axis_size("mp")
    tokens, depth = x.shape
    width = gate_weight.shape[1]
    w = 128 if width % 128 == 0 else width
    count = width // w
    vmem = pl.BlockSpec(memory_space=pltpu.VMEM)
    anywhere = pl.BlockSpec(memory_space=pl.ANY)
    dma = pltpu.SemaphoreType.DMA
    return pl.pallas_call(
        functools.partial(hidden_kernel, n, 3 if count > 1 else 1),
        in_specs=[vmem, vmem, anywhere, anywhere],
        out_specs=vmem,
        out_shape=jax.ShapeDtypeStruct((tokens, width), jnp.bfloat16),
        scratch_shapes=[
            pltpu.VMEM((2, depth, w), jnp.bfloat16),
            pltpu.VMEM((2, depth, w), jnp.bfloat16),
            pltpu.VMEM((count, 2, tokens, w), jnp.bfloat16),
            pltpu.VMEM((2, count, 2, tokens // 2, w), jnp.bfloat16),
            pltpu.VMEM((n, tokens // 2, 128), jnp.float32),
            dma((2, 2)),
            dma((2, count)),
            dma((2, count)),
            dma((2, count)),
            dma((2, count)),
            dma((2,)),
            dma((n,)),
        ],
        compiler_params=params(3),
    )(x, squares, gate_weight, up_weight)


def body(
    residual,
    query_states,
    key_states,
    value_states,
    prompt_perm,
    ablated_heads,
    out_weight,
    rms_gain,
    gate_weight,
    up_weight,
    down_weight,
):
    prompts_here, length, model_cols = residual.shape
    local_rows = prompts_here * length
    batches = lax.axis_size("batch")
    owned_cols = out_weight.shape[0]
    mine = owned_heads(query_states, key_states, value_states, owned_cols)
    prompts = batches * prompts_here
    mine = mine.reshape(prompts, length, owned_cols)
    head_of_col = (lax.axis_index("batch") * owned_cols + jnp.arange(owned_cols)) // HD
    chosen = jnp.any(head_of_col[:, None] == ablated_heads[None, :], axis=1)
    chosen = jnp.where(chosen, 1.0, 0.0).astype(jnp.float32)[None, :]
    ablated = swap(prompt_perm, chosen, mine).reshape(prompts * length, owned_cols)
    attn_part = jnp.dot(ablated, out_weight, preferred_element_type=jnp.float32)
    attn_out = scatter_sum(attn_part.astype(jnp.bfloat16).reshape(batches, local_rows, model_cols))
    hidden_state = residual.reshape(local_rows, model_cols).astype(jnp.float32) + attn_out.astype(
        jnp.float32
    )
    squares = jnp.sum(hidden_state * hidden_state, axis=1, keepdims=True)
    scaled = (hidden_state * rms_gain[None, :]).astype(jnp.bfloat16)
    block_rows, square_rows = gather_rows(scaled, jnp.broadcast_to(squares, (local_rows, 128)))
    block_rows = block_rows.reshape(batches * local_rows, model_cols)
    square_rows = square_rows.reshape(batches * local_rows, 128)
    hidden = hidden_rows(block_rows, square_rows, gate_weight, up_weight)
    mlp_part = jnp.dot(hidden, down_weight, preferred_element_type=jnp.float32)
    mlp_float = scatter_sum(mlp_part.astype(jnp.bfloat16).reshape(batches, local_rows, model_cols))
    return (
        attn_out.reshape(prompts_here, length, model_cols),
        mlp_float.reshape(prompts_here, length, model_cols),
    )


def solution(mesh):
    placed = (
        P("batch", None, "mp"),
        P("batch", None, "mp"),
        P("batch", None, None),
        P("batch", None, None),
        P(),
        P(),
        P("batch", "mp"),
        P("mp"),
        P("mp", "batch"),
        P("mp", "batch"),
        P("batch", "mp"),
    )
    return jax.shard_map(
        body,
        mesh=mesh,
        in_specs=placed,
        out_specs=(P("batch", None, "mp"), P("batch", None, "mp")),
        check_vma=False,
    )
```
